32 devices in a mesh: grp: 2 (over x), gx: 16 (over z, y, core).
Axes of the slice: x: 2, y: 2, z: 4, core: 2. Of those that a mesh axis runs over, the one named last changes fastest.
Arguments:
- state_field: bfloat16 [32, 64, 32768], P(None, 'gx', 'grp'), parts along dimension 2, may hold values from -6 to 6
- cotangent: bfloat16 [32, 64, 32768], P(None, 'gx', 'grp'), parts along dimension 2, may hold values from -6 to 6
- spectral_weight: bfloat16 [32, 1024, 1024], P(None, 'gx'), may hold values from -1 to 1
- local_weight: bfloat16 [32, 32], replicated, may hold values from -1 to 1
- local_bias: float32 [32], replicated, may hold values from -0.5 to 0.5
Outputs:
- layer_output: bfloat16 [32, 64, 32768], P(None, 'gx', 'grp'), parts along dimension 2
- field_grad: bfloat16 [32, 64, 32768], P(None, 'gx', 'grp'), parts along dimension 2
- spectral_grad: float32 [64, 1024, 1024], P('grp', 'gx'), parts along dimension 0
- local_weight_grad: float32 [64, 32], P('grp'), parts along dimension 0
- bias_grad: float32 [64], P('grp'), parts along dimension 0
The draws below stay inside these ranges and needn't reach their ends.
There are 2 independent parts, one for each index of `grp`. The reference program is written for one: setup_inputs(seed, part) draws one part's arguments, and reference() takes and returns one part's arrays. A program takes and returns all parts, laid end to end along the dimension named above; an argument that names none is the same for every part. Nothing has to cross between parts.
All inputs are finite; a program needn't handle non-finite values.
Results may differ from the reference program's by a relative error of at most 0.019.
Values may be sent and summed in bfloat16 or wider, within the bound.
No kernel may reach another device: no remote copies, remote signals or barrier semaphores. Data moves between devices by JAX's collectives and lax.ppermute only.
A program may use at most 192 MiB of HBM per device.

```python
import math
import jax
import jax.numpy as jnp
from jax import lax

C = 32
MODES = 16
K = 32
NY = 256
NZ = 64
NX = 64


def shard_levels(own_key, extent, pieces, smallest, high):
    def one(position, shards_of):
        draws = jax.random.uniform(jax.random.fold_in(jax.random.fold_in(own_key, 6), position), (shards_of,), jnp.float32, smallest / len(pieces), high / len(pieces))
        return jnp.repeat(jnp.exp(draws), extent[position] // shards_of).reshape((-1,) + (1,) * (len(extent) - position - 1))

    level = one(*pieces[0])
    for cut in pieces[1:]:
        level = level * one(*cut)
    return level


def noise(stream_key, shape, deviation, most, split=(), kind=jnp.bfloat16):
    values = deviation * jax.random.normal(stream_key, shape, jnp.float32)
    if split:
        values = values * shard_levels(stream_key, shape, split, -0.22, 0.18)
    return jnp.clip(values, -most, most).astype(kind)


def setup_inputs(seed: int = 0, part: int = 0) -> dict:
    keys = jax.random.split(jax.random.key(seed), 6)
    own_keys = jax.random.split(jax.random.fold_in(keys[5], part), 6)
    state_field = noise(own_keys[0], (C, NX, NY * NZ), 1.0, 6.0, ((1, 16),))
    cotangent = noise(own_keys[1], (C, NX, NY * NZ), 1.0, 6.0, ((1, 16),))
    spectral_weight = noise(keys[2], (K, K * K, C * C), C ** -0.5, 1.0, ((1, 16),))
    local_weight = noise(keys[3], (C, C), C ** -0.5, 1.0)
    local_bias = jnp.clip(jax.random.uniform(keys[4], (C,), jnp.float32, -0.5, 0.5), -0.5, 0.5)
    return dict(state_field=state_field, cotangent=cotangent, spectral_weight=spectral_weight, local_weight=local_weight, local_bias=local_bias)


def basis_table(length, mode_count):
    cells = jnp.arange(length, dtype=jnp.int32)
    rows = jnp.arange(2 * mode_count, dtype=jnp.int32)
    frequency = jnp.where(rows < mode_count, rows, rows - mode_count + 1)
    phase_index = frequency[:, None] * cells[None, :] % length
    angles = phase_index.astype(jnp.float32) * (2.0 * math.pi / length)
    cosine_rows = (rows < mode_count)[:, None]
    return jnp.where(cosine_rows, jnp.cos(angles), jnp.sin(angles)) * math.sqrt(2.0 / length)

def gelu_tanh(values_in):
    return jax.nn.gelu(values_in, approximate=True)

def project(values_in, table_x, table_y, table_z):
    highest = lax.Precision.HIGHEST
    section_one = jnp.einsum('cxyz,gz->cxyg', values_in.astype(jnp.float32), table_z.astype(jnp.float32), precision=highest)
    section_two = jnp.einsum('cxyg,by->cxbg', section_one, table_y, precision=highest)
    result = jnp.einsum('cxbg,ax->cabg', section_two, table_x, precision=highest)
    return result.reshape(result.shape[0], K, K * K)

def evaluate(mode_values, table_x, table_y, table_z):
    highest = lax.Precision.HIGHEST
    grid_modes = mode_values.astype(jnp.float32).reshape(mode_values.shape[0], K, K, K)
    section_one = jnp.einsum('cabg,ax->cxbg', grid_modes, table_x, precision=highest)
    section_two = jnp.einsum('cxbg,by->cxyg', section_one, table_y, precision=highest).astype(jnp.bfloat16)
    return jnp.einsum('cxyg,gz->cxyz', section_two.astype(jnp.float32), table_z.astype(jnp.float32), precision=highest)

def reference(state_field, cotangent, spectral_weight, local_weight, local_bias):
    highest = lax.Precision.HIGHEST
    state_grid = state_field.reshape(C, NX, NY, NZ)
    cotangent_grid = cotangent.reshape(C, NX, NY, NZ)
    table_x = basis_table(NX, MODES)
    table_y = basis_table(NY, MODES)
    table_z = basis_table(NZ, MODES).astype(jnp.bfloat16)
    weight_full = spectral_weight.astype(jnp.float32).reshape(K, K * K, C, C)
    coeffs = project(state_grid, table_x, table_y, table_z)
    mixed_coeffs = jnp.einsum('amco,cam->oam', weight_full, coeffs, precision=highest).astype(jnp.bfloat16)
    spectral_term = evaluate(mixed_coeffs, table_x, table_y, table_z)
    local_term = jnp.einsum('co,cxyz->oxyz', local_weight.astype(jnp.float32), state_grid.astype(jnp.float32), precision=highest)
    preact = spectral_term + local_term + local_bias.astype(jnp.float32)[:, None, None, None]
    layer_output, backward = jax.vjp(gelu_tanh, preact)
    hidden_grad = backward(cotangent_grid.astype(jnp.float32))[0].astype(jnp.bfloat16)
    hidden_full = hidden_grad.astype(jnp.float32)
    local_weight_grad = jnp.einsum('cxyz,oxyz->co', state_grid.astype(jnp.float32), hidden_full, precision=highest)
    bias_grad = lax.optimization_barrier(jnp.sum(hidden_full, axis=(1, 2, 3)))
    grad_coeffs = project(hidden_grad, table_x, table_y, table_z)
    coeffs_moved = jnp.transpose(coeffs, (1, 2, 0))
    grads_moved = jnp.transpose(grad_coeffs, (1, 2, 0))
    spectral_grad = (coeffs_moved[:, :, :, None] * grads_moved[:, :, None, :]).reshape(K, K * K, C * C)
    back_modes = jnp.einsum('amco,oam->cam', weight_full, grad_coeffs, precision=highest).astype(jnp.bfloat16)
    local_back = jnp.einsum('co,oxyz->cxyz', local_weight.astype(jnp.float32), hidden_full, precision=highest)
    field_grad = (local_back + evaluate(back_modes, table_x, table_y, table_z)).astype(jnp.bfloat16)
    return (layer_output.astype(jnp.bfloat16).reshape(C, NX, NY * NZ), field_grad.reshape(C, NX, NY * NZ), spectral_grad, local_weight_grad, bias_grad)
```

```python
import functools
import math

import jax
import jax.numpy as jnp
import numpy as np
from jax import lax
from jax.experimental import pallas as pl
from jax.experimental.pallas import tpu as pltpu
from jax.sharding import PartitionSpec as P

MODES = 16
K = 2 * MODES
NZ = 64
YC = 4
CHUNK = YC * NZ
AG = 4
F32 = jnp.float32
BF16 = jnp.bfloat16
NN = (((1,), (0,)), ((), ()))
NT = (((1,), (1,)), ((), ()))


def dot(lhs, rhs, dims=NN, precision=None):
    return lax.dot_general(lhs, rhs, dims, precision=precision, preferred_element_type=F32)


def basis_table(length):
    cells = np.arange(length)
    rows = np.arange(K)
    frequency = np.where(rows < MODES, rows, rows - MODES + 1)
    phase_index = frequency[:, None] * cells[None, :] % length
    angles = phase_index.astype(np.float32) * np.float32(2.0 * math.pi / length)
    angles = angles.astype(np.float64)
    table = np.where((rows < MODES)[:, None], np.cos(angles), np.sin(angles))
    return (table * math.sqrt(2.0 / length)).astype(np.float32)


def halves(table):
    high = table.astype(BF16)
    low = (table - high.astype(np.float32)).astype(BF16)
    return high, low


def tables(channels, rows_x, devices, cells_y):
    table_x = basis_table(rows_x * devices)
    y_high, y_low = halves(basis_table(cells_y))
    z = basis_table(NZ).astype(BF16).astype(np.float32)
    eye_c = np.eye(channels, dtype=np.float32)
    out = {}
    out["z"] = np.kron(np.eye(YC, dtype=np.float32), z).astype(BF16)
    out["y"] = np.concatenate([y_high, y_low], 0)
    out["yt"] = np.concatenate([y_high.T, y_low.T], 1)
    out["eye"] = np.eye(channels * rows_x, dtype=np.float32).astype(BF16)
    out["rep"] = np.kron(eye_c, np.ones((rows_x, 1), np.float32)).astype(BF16)
    groups = K // AG
    x_high, x_low = halves(table_x)
    kx = np.stack([x_high, x_low]).astype(np.float32)
    kx = kx.reshape(2, groups, AG, devices, rows_x)
    kx = np.einsum("htadx,ce->thacdex", kx, eye_c)
    out["x"] = kx.reshape(
        groups, 2 * AG * channels, devices * channels * rows_x
    ).astype(BF16)
    eye_a = np.eye(AG, dtype=np.float32)
    ones = np.ones(channels, np.float32)
    sel_c = np.einsum("ab,ce,o->abceo", eye_a, eye_c, ones)
    sel_c = sel_c.reshape(AG, AG * channels, channels * channels)
    out["sel_c"] = np.concatenate([sel_c, sel_c], 1).astype(BF16)
    sel_o = np.einsum("ab,c,eo->abeco", eye_a, ones, eye_c)
    sel_o = sel_o.reshape(AG, AG * channels, channels * channels)
    out["sel_o"] = np.concatenate([sel_o, sel_o], 1).astype(BF16)
    c_low = 128 // channels
    fold_c = np.einsum("ab,c,oe->acobe", eye_a, np.ones(c_low, np.float32), eye_c)
    fold_c = fold_c.reshape(AG, 128, AG * channels)
    out["fold_c"] = np.concatenate([fold_c, fold_c], 1).reshape(
        AG * 256, AG * channels
    ).astype(BF16)
    fold_o = np.einsum("ab,ce,o->acobe", eye_a, eye_c, ones)
    out["fold_o"] = fold_o.reshape(AG, channels * channels, AG * channels).astype(BF16)
    return {name: jnp.asarray(value) for name, value in out.items()}


def split(values_in):
    high = values_in.astype(BF16)
    low = (values_in - high.astype(F32)).astype(BF16)
    return jnp.concatenate([high, low], 1)


def contract_y(p1_ref, y_ref, sums_ref, out_ref, cells_y):
    y = y_ref[...]
    width = p1_ref.shape[1]
    for g in range(0, K, 2):
        pair = [p1_ref[pl.ds(g + i, cells_y, stride=K), :].astype(BF16) for i in range(2)]
        both = dot(y, jnp.concatenate(pair, 1))
        both = both[:K] + both[K:]
        for i in range(2):
            sums_ref[pl.ds(g + i, K, stride=K), :] = both[:, i * width : (i + 1) * width]
    out_ref[...] = sums_ref[...].astype(BF16)


def expand_y(e1_ref, yt_ref, sums_ref, e2_ref, cells_y):
    sums_ref[...] = e1_ref[...].astype(F32)
    yt = yt_ref[...]
    width = e1_ref.shape[1]
    for g in range(0, K, 2):
        pair = [sums_ref[pl.ds(g + i, K, stride=K), :].astype(BF16) for i in range(2)]
        rhs = jnp.concatenate(pair, 1)
        both = dot(yt, jnp.concatenate([rhs, rhs], 0))
        for i in range(2):
            e2_ref[pl.ds(g + i, cells_y, stride=K), :] = both[:, i * width : (i + 1) * width]


def spread_weight(rep_ref, weight):
    rep = rep_ref[...]
    wide = dot(dot(rep, weight).astype(BF16), rep, NT)
    rows_x = rep.shape[0] // rep.shape[1]
    row = lax.broadcasted_iota(jnp.int32, wide.shape, 0)
    col = lax.broadcasted_iota(jnp.int32, wide.shape, 1)
    return jnp.where(row % rows_x == col % rows_x, wide, 0.0).astype(BF16)


def project_kernel(state_ref, z_ref, y_ref, out_ref, p1_ref, sums_ref, *, chunks, cells_y):
    step = pl.program_id(0)
    z = z_ref[...]
    rows = z.shape[0]
    for j in range(chunks):
        cells = state_ref[:, :, j * CHUNK : (j + 1) * CHUNK].reshape(-1, CHUNK)
        p1_ref[pl.ds((step * chunks + j) * rows, rows), :] = dot(z, cells, NT)

    @pl.when(step == pl.num_programs(0) - 1)
    def _():
        contract_y(p1_ref, y_ref, sums_ref, out_ref, cells_y)


def mix_kernel(got_ref, weight_ref, x_ref, sel_ref, fold_ref, send_ref, coeffs_ref, flat_ref, total_ref, *, devices):
    step = pl.program_id(0)
    width = got_ref.shape[2]

    @pl.when(step == 0)
    def _():
        for d in range(devices):
            flat_ref[:, d * width : (d + 1) * width] = got_ref[d]
        total_ref[...] = jnp.zeros_like(total_ref)

    x = x_ref[0]
    both = dot(flat_ref[...], x, NT)
    coeffs = both[:, : both.shape[1] // 2] + both[:, both.shape[1] // 2 :]
    coeffs_ref[...] = coeffs
    left = split(coeffs)
    parts = []
    for a in range(AG):
        product = dot(left, sel_ref[a]) * weight_ref[a].astype(F32)
        pieces = [product[:, i * 128 : (i + 1) * 128] for i in range(product.shape[1] // 128)]
        while len(pieces) > 1:
            pieces = [pieces[i] + pieces[i + 1] for i in range(0, len(pieces), 2)]
        parts.append(split(pieces[0]))
    mixed = dot(jnp.concatenate(parts, 1), fold_ref[...]).astype(BF16)
    total_ref[...] += dot(jnp.concatenate([mixed, mixed], 1), x)

    @pl.when(step == pl.num_programs(0) - 1)
    def _():
        for d in range(devices):
            send_ref[d] = total_ref[:, d * width : (d + 1) * width].astype(BF16)


def mode_grad_kernel(
    got_ref, weight_ref, coeffs_ref, x_ref, sel_c_ref, sel_o_ref, fold_ref,
    send_ref, spectral_ref, flat_ref, total_ref, *, devices,
):
    step = pl.program_id(0)
    width = got_ref.shape[2]

    @pl.when(step == 0)
    def _():
        for d in range(devices):
            flat_ref[:, d * width : (d + 1) * width] = got_ref[d]
        total_ref[...] = jnp.zeros_like(total_ref)

    x = x_ref[0]
    both = dot(flat_ref[...], x, NT)
    grads = both[:, : both.shape[1] // 2] + both[:, both.shape[1] // 2 :]
    grads = split(grads)
    coeffs = split(coeffs_ref[...])
    back = jnp.zeros((flat_ref.shape[0], width), F32)
    for a in range(AG):
        grads_wide = dot(grads, sel_o_ref[a])
        spectral_ref[a] = dot(coeffs, sel_c_ref[a]) * grads_wide
        product = (grads_wide * weight_ref[a].astype(F32)).astype(BF16)
        back = back + dot(product, fold_ref[a])
    back = back.astype(BF16)
    total_ref[...] += dot(jnp.concatenate([back, back], 1), x)

    @pl.when(step == pl.num_programs(0) - 1)
    def _():
        for d in range(devices):
            send_ref[d] = total_ref[:, d * width : (d + 1) * width].astype(BF16)


GELU_A = math.sqrt(2.0 / math.pi)
GELU_B = GELU_A * 0.044715


def layer_kernel(
    got_ref, state_ref, cotangent_ref, weight_ref, bias_ref, z_ref, y_ref, yt_ref, eye_ref, rep_ref,
    output_ref, hidden_ref, send_ref, local_ref,
    e2_ref, p1_ref, sums_ref, mix_ref, bias_wide_ref, acc_ref, *, chunks, cells_y,
):
    step = pl.program_id(0)
    rows = z_ref.shape[0]
    width = rep_ref.shape[0]

    @pl.when(step == 0)
    def _():
        expand_y(got_ref, yt_ref, sums_ref, e2_ref, cells_y)
        mix_ref[...] = spread_weight(rep_ref, weight_ref[...].astype(F32).T.astype(BF16))
        bias = jnp.sum(rep_ref[...].astype(F32) * bias_ref[...], axis=1, keepdims=True)
        bias_wide_ref[...] = jnp.broadcast_to(bias, bias_wide_ref.shape)
        acc_ref[...] = jnp.zeros_like(acc_ref)

    z = z_ref[...]
    ones = jnp.ones((16, CHUNK), BF16)
    bias = jnp.concatenate([bias_wide_ref[...]] * (CHUNK // 128), 1)
    acc = acc_ref[...]
    for j in range(chunks):
        lanes = slice(j * CHUNK, (j + 1) * CHUNK)
        place = pl.ds((step * chunks + j) * rows, rows)
        cells = state_ref[:, :, lanes].reshape(-1, CHUNK)
        e2 = dot(eye_ref[...], e2_ref[place, :].astype(BF16), NT).astype(BF16)
        left = jnp.concatenate([e2, mix_ref[...]], 1)
        pre = dot(left, jnp.concatenate([z, cells], 0)) + bias
        square = pre * pre
        half = 0.5 * jnp.tanh(pre * (GELU_A + GELU_B * square)) + 0.5
        output_ref[:, :, lanes] = (pre * half).astype(BF16).reshape(-1, state_ref.shape[1], CHUNK)
        slope = half + (half - half * half) * (pre * (2 * GELU_A + 6 * GELU_B * square))
        cot = cotangent_ref[:, :, lanes].reshape(-1, CHUNK).astype(F32)
        hidden = (cot * slope).astype(BF16)
        hidden_ref[:, lanes] = hidden
        sums = dot(jnp.concatenate([z, cells, ones], 0), hidden, NT)
        p1_ref[place, :] = sums[:rows]
        acc = acc + sums[rows:]
    acc_ref[...] = acc

    @pl.when(step == pl.num_programs(0) - 1)
    def _():
        contract_y(p1_ref, y_ref, sums_ref, send_ref, cells_y)
        rows_x = width // rep_ref.shape[1]
        full = acc_ref[:width]
        row = lax.broadcasted_iota(jnp.int32, full.shape, 0)
        col = lax.broadcasted_iota(jnp.int32, full.shape, 1)
        full = jnp.where(row % rows_x == col % rows_x, full, 0.0)
        rep = rep_ref[...].astype(F32)
        high = lax.Precision.HIGHEST
        tall = dot(jnp.concatenate([full, acc_ref[width : width + 8]], 0), rep, precision=high)
        local_ref[: rep.shape[1]] = dot(rep.T, tall[:width], precision=high)
        local_ref[rep.shape[1] :] = tall[width:]


def field_grad_kernel(
    got_ref, hidden_ref, weight_ref, z_ref, yt_ref, eye_ref, rep_ref, output_ref, e2_ref, sums_ref, mix_ref,
    *, chunks, cells_y,
):
    step = pl.program_id(0)
    rows = z_ref.shape[0]

    @pl.when(step == 0)
    def _():
        expand_y(got_ref, yt_ref, sums_ref, e2_ref, cells_y)
        mix_ref[...] = spread_weight(rep_ref, weight_ref[...])

    z = z_ref[...]
    for j in range(chunks):
        lanes = slice(j * CHUNK, (j + 1) * CHUNK)
        place = pl.ds((step * chunks + j) * rows, rows)
        e2 = dot(eye_ref[...], e2_ref[place, :].astype(BF16), NT).astype(BF16)
        left = jnp.concatenate([e2, mix_ref[...]], 1)
        grad = dot(left, jnp.concatenate([z, hidden_ref[:, lanes]], 0))
        output_ref[:, :, lanes] = grad.astype(BF16).reshape(-1, output_ref.shape[1], CHUNK)


def whole(array):
    return pl.BlockSpec(array.shape, lambda i: (0,) * array.ndim)


def body(state_field, cotangent, spectral_weight, local_weight, local_bias):
    channels, rows_x, cells = state_field.shape
    cells_y = cells // NZ
    devices = lax.axis_size("gx")
    mode_rows = spectral_weight.shape[1]
    wide = channels * rows_x
    groups = K // AG
    table = tables(channels, rows_x, devices, cells_y)
    steps = 8
    lanes = cells // steps
    chunks = lanes // CHUNK
    params = pltpu.CompilerParams(
        dimension_semantics=("arbitrary",), vmem_limit_bytes=28 * 1024 * 1024
    )
    field_spec = pl.BlockSpec((channels, rows_x, lanes), lambda i: (0, 0, i))
    flat_spec = pl.BlockSpec((wide, lanes), lambda i: (0, i))
    modes = jax.ShapeDtypeStruct((K * K, wide), BF16)
    modes_spec = pl.BlockSpec(modes.shape, lambda i: (0, 0))
    blocks = jax.ShapeDtypeStruct((devices, mode_rows, wide), BF16)
    blocks_spec = pl.BlockSpec(blocks.shape, lambda i: (0, 0, 0))
    weight_spec = pl.BlockSpec((AG, mode_rows, channels * channels), lambda i: (i, 0, 0))
    x_spec = pl.BlockSpec((1,) + table["x"].shape[1:], lambda i: (i, 0, 0))
    coeffs_spec = pl.BlockSpec((mode_rows, AG * channels), lambda i: (0, i))
    p1 = pltpu.VMEM((cells_y * K, wide), F32)
    sums = pltpu.VMEM((K * K, wide), F32)
    flat = pltpu.VMEM((mode_rows, devices * wide), BF16)
    total = pltpu.VMEM((mode_rows, devices * wide), F32)

    def exchange(values_in):
        sent = values_in.reshape(blocks.shape)
        return lax.all_to_all(sent, "gx", 0, 0, tiled=True)

    projected = pl.pallas_call(
        functools.partial(project_kernel, chunks=chunks, cells_y=cells_y),
        grid=(steps,),
        in_specs=[field_spec, whole(table["z"]), whole(table["y"])],
        out_specs=modes_spec,
        out_shape=modes,
        scratch_shapes=[p1, sums],
        compiler_params=params,
        name="project",
    )(state_field, table["z"], table["y"])
    got = exchange(projected)
    mixed, coeffs = pl.pallas_call(
        functools.partial(mix_kernel, devices=devices),
        grid=(groups,),
        in_specs=[blocks_spec, weight_spec, x_spec, whole(table["sel_c"]), whole(table["fold_c"])],
        out_specs=[blocks_spec, coeffs_spec],
        out_shape=[blocks, jax.ShapeDtypeStruct((mode_rows, K * channels), F32)],
        scratch_shapes=[flat, total],
        compiler_params=params,
        name="mix",
    )(got, spectral_weight, table["x"], table["sel_c"], table["fold_c"])
    got = exchange(mixed).reshape(modes.shape)
    bias_row = local_bias.reshape(1, channels)
    layer_output, hidden, projected, local = pl.pallas_call(
        functools.partial(layer_kernel, chunks=chunks, cells_y=cells_y),
        grid=(steps,),
        in_specs=[
            modes_spec, field_spec, field_spec, whole(local_weight), whole(bias_row),
            whole(table["z"]), whole(table["y"]), whole(table["yt"]), whole(table["eye"]), whole(table["rep"]),
        ],
        out_specs=[
            field_spec, flat_spec, modes_spec,
            pl.BlockSpec((channels + 8, channels), lambda i: (0, 0)),
        ],
        out_shape=[
            jax.ShapeDtypeStruct(state_field.shape, BF16),
            jax.ShapeDtypeStruct((wide, cells), BF16),
            modes,
            jax.ShapeDtypeStruct((channels + 8, channels), F32),
        ],
        scratch_shapes=[
            p1, p1, sums, pltpu.VMEM((wide, wide), BF16),
            pltpu.VMEM((wide, 128), F32), pltpu.VMEM((wide + 16, wide), F32),
        ],
        compiler_params=params,
        name="layer",
    )(
        got, state_field, cotangent, local_weight, bias_row,
        table["z"], table["y"], table["yt"], table["eye"], table["rep"],
    )
    local = jnp.sum(lax.all_gather(local, "gx", axis=0, tiled=False), axis=0)
    got = exchange(projected)
    back, spectral_grad = pl.pallas_call(
        functools.partial(mode_grad_kernel, devices=devices),
        grid=(groups,),
        in_specs=[
            blocks_spec, weight_spec, coeffs_spec, x_spec,
            whole(table["sel_c"]), whole(table["sel_o"]), whole(table["fold_o"]),
        ],
        out_specs=[blocks_spec, weight_spec],
        out_shape=[blocks, jax.ShapeDtypeStruct(spectral_weight.shape, F32)],
        scratch_shapes=[flat, total],
        compiler_params=params,
        name="mode_grad",
    )(got, spectral_weight, coeffs, table["x"], table["sel_c"], table["sel_o"], table["fold_o"])
    got = exchange(back).reshape(modes.shape)
    field_grad = pl.pallas_call(
        functools.partial(field_grad_kernel, chunks=chunks, cells_y=cells_y),
        grid=(steps,),
        in_specs=[
            modes_spec, flat_spec, whole(local_weight),
            whole(table["z"]), whole(table["yt"]), whole(table["eye"]), whole(table["rep"]),
        ],
        out_specs=field_spec,
        out_shape=jax.ShapeDtypeStruct(state_field.shape, BF16),
        scratch_shapes=[p1, sums, pltpu.VMEM((wide, wide), BF16)],
        compiler_params=params,
        name="field_grad",
    )(got, hidden, local_weight, table["z"], table["yt"], table["eye"], table["rep"])
    return (layer_output, field_grad, spectral_grad, local[:channels], local[channels])


def solution(mesh):
    placed = (P(None, "gx", "grp"), P(None, "gx", "grp"), P(None, "gx", None), P(), P())
    return jax.shard_map(
        body,
        mesh=mesh,
        in_specs=placed,
        out_specs=(
            P(None, "gx", "grp"),
            P(None, "gx", "grp"),
            P("grp", "gx", None),
            P("grp", None),
            P("grp"),
        ),
        check_vma=False,
    )
```

```python
import functools
import math

import jax
import jax.numpy as jnp
import numpy as np
from jax import lax
from jax.experimental import pallas as pl
from jax.experimental.pallas import tpu as pltpu
from jax.sharding import PartitionSpec as P

MODES = 16
K = 2 * MODES
NZ = 64
YC = 4
CHUNK = YC * NZ
AG = 4
PITCH = K + 1
PACK = 32
F32 = jnp.float32
BF16 = jnp.bfloat16
NN = (((1,), (0,)), ((), ()))
NT = (((1,), (1,)), ((), ()))


def dot(lhs, rhs, dims=NN, precision=None):
    return lax.dot_general(lhs, rhs, dims, precision=precision, preferred_element_type=F32)


def basis_table(length):
    cells = np.arange(length)
    rows = np.arange(K)
    frequency = np.where(rows < MODES, rows, rows - MODES + 1)
    phase_index = frequency[:, None] * cells[None, :] % length
    angles = phase_index.astype(np.float32) * np.float32(2.0 * math.pi / length)
    angles = angles.astype(np.float64)
    table = np.where((rows < MODES)[:, None], np.cos(angles), np.sin(angles))
    return (table * math.sqrt(2.0 / length)).astype(np.float32)


def halves(table):
    high = table.astype(BF16)
    low = (table - high.astype(np.float32)).astype(BF16)
    return high, low


def tables(channels, rows_x, devices, cells_y):
    table_x = basis_table(rows_x * devices)
    y_high, y_low = halves(basis_table(cells_y))
    z = basis_table(NZ).astype(BF16).astype(np.float32)
    eye_c = np.eye(channels, dtype=np.float32)
    out = {}
    out["z"] = np.kron(np.eye(YC, dtype=np.float32), z).astype(BF16)
    out["y"] = np.concatenate([y_high, y_low], 0)
    out["yt"] = np.concatenate([y_high.T, y_low.T], 1)
    out["eye"] = np.eye(channels * rows_x, dtype=np.float32).astype(BF16)
    out["rep"] = np.kron(eye_c, np.ones((rows_x, 1), np.float32)).astype(BF16)
    kx = table_x.reshape(K, devices, rows_x)
    kx = np.einsum("adx,ce->acdex", kx, eye_c)
    out["x"] = kx.reshape(K * channels, devices * channels * rows_x).astype(BF16)
    eye_a = np.eye(AG, dtype=np.float32)
    ones = np.ones(channels, np.float32)
    tile = 128 // channels
    sel_c = np.einsum("ab,ce,o->abceo", eye_a, eye_c, ones)
    sel_c = sel_c.reshape(AG, AG * channels, channels * channels)
    out["sel_c"] = np.concatenate([sel_c, sel_c], 1).astype(BF16)
    sel_o = np.einsum("ab,c,eo->abeco", eye_a, np.ones(tile, np.float32), eye_c)
    sel_o = sel_o.reshape(AG, AG * channels, 128)
    out["sel_o"] = np.concatenate([sel_o, sel_o], 1).astype(BF16)
    fold_c = np.einsum("ab,c,oe->acobe", eye_a, np.ones(tile, np.float32), eye_c)
    fold_c = fold_c.reshape(AG, 128, AG * channels)
    out["fold_c"] = np.concatenate([fold_c, fold_c], 1).reshape(
        AG * 256, AG * channels
    ).astype(BF16)
    fold_o = np.einsum("ab,ce,o->acobe", eye_a, eye_c, ones)
    out["fold_o"] = fold_o.reshape(AG, channels * channels, AG * channels).astype(BF16)
    return {name: jnp.asarray(value) for name, value in out.items()}


def split(values_in):
    high = values_in.astype(BF16)
    low = (values_in - high.astype(F32)).astype(BF16)
    return jnp.concatenate([high, low], 1)


def put_chunk(ref, index, values_in):
    for i in range(YC):
        ref[pl.ds((index * YC + i) * PITCH, K), :] = values_in[i * K : (i + 1) * K]


def take_chunk(ref, index):
    parts = [ref[pl.ds((index * YC + i) * PITCH, K), :] for i in range(YC)]
    return jnp.concatenate(parts, 0).astype(BF16)


def contract_y(p1_ref, y_ref, sums_ref, cells_y):
    y = y_ref[...]
    width = p1_ref.shape[1]
    for g in range(0, K, 2):
        pair = [p1_ref[pl.ds(g + i, cells_y, stride=PITCH), :].astype(BF16) for i in range(2)]
        both = dot(y, jnp.concatenate(pair, 1))
        both = both[:K] + both[K:]
        for i in range(2):
            sums_ref[pl.ds(g + i, K, stride=PITCH), :] = both[:, i * width : (i + 1) * width]


def block_of(sums_ref, index, mode_rows):
    first = index * (mode_rows // K)
    parts = [sums_ref[(first + i) * PITCH : (first + i) * PITCH + K, :] for i in range(mode_rows // K)]
    return jnp.concatenate(parts, 0).astype(BF16)


def expand_y(got_ref, yt_ref, sums_ref, e2_ref, cells_y):
    devices, mode_rows, width = got_ref.shape
    for d in range(devices):
        block = got_ref[d].astype(F32)
        for i in range(mode_rows // K):
            first = (d * (mode_rows // K) + i) * PITCH
            sums_ref[first : first + K, :] = block[i * K : (i + 1) * K]
    yt = yt_ref[...]
    for g in range(0, K, 2):
        pair = [sums_ref[pl.ds(g + i, K, stride=PITCH), :].astype(BF16) for i in range(2)]
        rhs = jnp.concatenate(pair, 1)
        both = dot(yt, jnp.concatenate([rhs, rhs], 0))
        for i in range(2):
            e2_ref[pl.ds(g + i, cells_y, stride=PITCH), :] = both[:, i * width : (i + 1) * width]


def spread_weight(rep_ref, weight):
    rep = rep_ref[...]
    wide = dot(dot(rep, weight).astype(BF16), rep, NT)
    rows_x = rep.shape[0] // rep.shape[1]
    row = lax.broadcasted_iota(jnp.int32, wide.shape, 0)
    col = lax.broadcasted_iota(jnp.int32, wide.shape, 1)
    return jnp.where(row % rows_x == col % rows_x, wide, 0.0).astype(BF16)


def project_kernel(state_ref, z_ref, y_ref, out_ref, p1_ref, sums_ref, *, chunks, cells_y):
    step = pl.program_id(0)
    z = z_ref[...]
    for j in range(chunks):
        cells = state_ref[:, :, j * CHUNK : (j + 1) * CHUNK].reshape(-1, CHUNK)
        put_chunk(p1_ref, step * chunks + j, dot(z, cells, NT))

    @pl.when(step == pl.num_programs(0) - 1)
    def _():
        contract_y(p1_ref, y_ref, sums_ref, cells_y)
        devices, mode_rows, _ = out_ref.shape
        for d in range(devices):
            out_ref[d] = block_of(sums_ref, d, mode_rows)


def sum_x(got_ref, x_ref, coeffs_ref, mode_rows):
    devices, _, width = got_ref.shape
    flat = jnp.concatenate([got_ref[d, :mode_rows] for d in range(devices)], 1)
    coeffs = dot(flat, x_ref[...], NT)
    for t in range(K // AG):
        coeffs_ref[t * mode_rows : (t + 1) * mode_rows, :] = coeffs[:, t * width : (t + 1) * width]


def spread_x(modes, x_ref, send_ref):
    devices, mode_rows, width = send_ref.shape
    flat = jnp.concatenate([modes[t * mode_rows : (t + 1) * mode_rows] for t in range(K // AG)], 1)
    values = dot(flat, x_ref[...])
    for d in range(devices):
        send_ref[d] = values[:, d * width : (d + 1) * width].astype(BF16)


def mix_kernel(got_ref, weight_ref, x_ref, sel_ref, fold_ref, send_ref, coeffs_ref):
    mode_rows, pairs = weight_ref.shape[2:]
    rows = coeffs_ref.shape[0]
    sum_x(got_ref, x_ref, coeffs_ref, mode_rows)
    left = split(coeffs_ref[...])
    parts = []
    for a in range(AG):
        total = None
        for q in range(0, pairs, 256):
            weight = weight_ref[:, a, :, q : q + 256].reshape(rows, 256).astype(F32)
            product = dot(left, sel_ref[a, :, q : q + 256]) * weight
            product = product[:, :128] + product[:, 128:]
            total = product if total is None else total + product
        parts.append(split(total))
    mixed = dot(jnp.concatenate(parts, 1), fold_ref[...]).astype(BF16)
    spread_x(mixed, x_ref, send_ref)


def back_kernel(got_ref, weight_ref, x_ref, sel_ref, fold_ref, send_ref, grads_ref, local_ref):
    mode_rows, pairs = weight_ref.shape[2:]
    rows = grads_ref.shape[0]
    sum_x(got_ref, x_ref, grads_ref, mode_rows)
    left = split(grads_ref[...])
    back = jnp.zeros(grads_ref.shape, F32)
    for a in range(AG):
        grads = dot(left, sel_ref[a])
        grads = jnp.concatenate([grads, grads], 1)
        for q in range(0, pairs, 256):
            weight = weight_ref[:, a, :, q : q + 256].reshape(rows, 256).astype(F32)
            back = back + dot((grads * weight).astype(BF16), fold_ref[a, q : q + 256, :])
    spread_x(back.astype(BF16), x_ref, send_ref)
    local = got_ref[0, mode_rows:].astype(F32)
    for d in range(1, got_ref.shape[0]):
        local = local + got_ref[d, mode_rows:].astype(F32)
    width = local.shape[1] // 4
    local_ref[0] = local[:, :width] + local[:, width : 2 * width]
    local_ref[1] = local[:, 2 * width : 3 * width] + local[:, 3 * width :]


def spectral_kernel(coeffs_ref, grads_ref, sel_c_ref, sel_o_ref, out_ref):
    groups, _, mode_rows, pairs = out_ref.shape
    coeffs = split(coeffs_ref[...])
    grads = dot(split(grads_ref[...]), sel_o_ref[0])
    grads = jnp.concatenate([grads, grads], 1)
    for q in range(0, pairs, 256):
        product = dot(coeffs, sel_c_ref[0, :, q : q + 256]) * grads
        out_ref[:, 0, :, q : q + 256] = product.reshape(groups, mode_rows, 256)


GELU_A = math.sqrt(2.0 / math.pi)
GELU_B = GELU_A * 0.044715


def staged(count, stages):
    held = {}
    for tick in range(count + len(stages) - 1):
        for index, stage in enumerate(stages):
            item = tick - index
            if 0 <= item < count:
                held[item] = stage(item, held.get(item))


def layer_kernel(
    got_ref, state_ref, cotangent_ref, weight_ref, bias_ref, z_ref, y_ref, yt_ref, eye_ref, rep_ref,
    output_ref, hidden_ref, send_ref,
    e2_ref, p1_ref, sums_ref, mix_ref, bias_wide_ref, acc_ref, *, chunks, cells_y,
):
    step = pl.program_id(0)
    rows = z_ref.shape[0]
    width = rep_ref.shape[0]
    rows_x = state_ref.shape[1]

    @pl.when(step == 0)
    def _():
        expand_y(got_ref, yt_ref, sums_ref, e2_ref, cells_y)
        mix_ref[...] = spread_weight(rep_ref, weight_ref[...].astype(F32).T.astype(BF16))
        bias = jnp.sum(rep_ref[...].astype(F32) * bias_ref[...], axis=1, keepdims=True)
        bias_wide_ref[...] = jnp.broadcast_to(bias, bias_wide_ref.shape)
        acc_ref[...] = jnp.zeros_like(acc_ref)

    z = z_ref[...]
    ones = jnp.ones((16, CHUNK), BF16)
    bias = jnp.concatenate([bias_wide_ref[...]] * (CHUNK // 128), 1)
    acc = [acc_ref[...]]

    def lanes(j):
        return pl.ds(pl.multiple_of((step * chunks + j) * CHUNK, CHUNK), CHUNK)

    def cells(j):
        return state_ref[:, :, lanes(j)].reshape(-1, CHUNK)

    def turn(j, _):
        return dot(eye_ref[...], take_chunk(e2_ref, step * chunks + j), NT).astype(BF16)

    def evaluate(j, e2):
        left = jnp.concatenate([e2, mix_ref[...]], 1)
        return dot(left, jnp.concatenate([z, cells(j)], 0)) + bias

    def activate(j, pre):
        square = pre * pre
        half = 0.5 * jnp.tanh(pre * (GELU_A + GELU_B * square)) + 0.5
        own = slice(j * CHUNK, (j + 1) * CHUNK)
        output_ref[:, :, own] = (pre * half).astype(BF16).reshape(-1, rows_x, CHUNK)
        slope = half + (half - half * half) * (pre * (2 * GELU_A + 6 * GELU_B * square))
        cot = cotangent_ref[:, :, lanes(j)].reshape(-1, CHUNK).astype(F32)
        hidden = (cot * slope).astype(BF16)
        hidden_ref[:, lanes(j)] = hidden
        return hidden

    def reduce(j, hidden):
        sums = dot(jnp.concatenate([z, cells(j), ones], 0), hidden, NT)
        put_chunk(p1_ref, step * chunks + j, sums[:rows])
        acc[0] = acc[0] + sums[rows:]

    staged(chunks, [turn, evaluate, activate, reduce])
    acc_ref[...] = acc[0]

    @pl.when(step == pl.num_programs(0) - 1)
    def _():
        contract_y(p1_ref, y_ref, sums_ref, cells_y)
        full = acc_ref[:width]
        row = lax.broadcasted_iota(jnp.int32, full.shape, 0)
        col = lax.broadcasted_iota(jnp.int32, full.shape, 1)
        full = jnp.where(row % rows_x == col % rows_x, full, 0.0)
        rep = rep_ref[...].astype(F32)
        high = lax.Precision.HIGHEST
        tall = dot(jnp.concatenate([full, acc_ref[width : width + 8]], 0), rep, precision=high)
        channels = rep.shape[1]
        local = dot(rep.T, tall[:width], precision=high)
        bias_sum = jnp.broadcast_to(tall[width : width + 1], (channels, channels))
        packed = jnp.concatenate([split(local), split(bias_sum)], 1)
        devices = send_ref.shape[0]
        mode_rows = K * K // devices
        for d in range(devices):
            send_ref[d, :mode_rows] = block_of(sums_ref, d, mode_rows)
            send_ref[d, mode_rows:] = packed


def field_grad_kernel(
    got_ref, hidden_ref, weight_ref, z_ref, yt_ref, eye_ref, rep_ref, output_ref, e2_ref, sums_ref, mix_ref,
    *, chunks, cells_y,
):
    step = pl.program_id(0)

    @pl.when(step == 0)
    def _():
        expand_y(got_ref, yt_ref, sums_ref, e2_ref, cells_y)
        mix_ref[...] = spread_weight(rep_ref, weight_ref[...])

    z = z_ref[...]

    def turn(j, _):
        return dot(eye_ref[...], take_chunk(e2_ref, step * chunks + j), NT).astype(BF16)

    def evaluate(j, e2):
        left = jnp.concatenate([e2, mix_ref[...]], 1)
        start = pl.multiple_of((step * chunks + j) * CHUNK, CHUNK)
        grad = dot(left, jnp.concatenate([z, hidden_ref[:, pl.ds(start, CHUNK)]], 0))
        own = slice(j * CHUNK, (j + 1) * CHUNK)
        output_ref[:, :, own] = grad.astype(BF16).reshape(-1, output_ref.shape[1], CHUNK)

    staged(chunks, [turn, evaluate])


def body(state_field, cotangent, spectral_weight, local_weight, local_bias):
    channels, rows_x, cells = state_field.shape
    cells_y = cells // NZ
    devices = lax.axis_size("gx")
    mode_rows = spectral_weight.shape[1]
    wide = channels * rows_x
    groups = K // AG
    table = tables(channels, rows_x, devices, cells_y)
    steps = 8
    lanes = cells // steps
    chunks = lanes // CHUNK
    in_vmem = pl.BlockSpec(memory_space=pltpu.VMEM)

    def params(mib):
        return pltpu.CompilerParams(vmem_limit_bytes=mib * 1024 * 1024)

    def whole(array):
        return pl.BlockSpec(array.shape, lambda i: (0,) * len(array.shape))

    field_spec = pl.BlockSpec((channels, rows_x, lanes), lambda i: (0, 0, i))
    blocks = jax.ShapeDtypeStruct((devices, mode_rows, wide), BF16)
    packed = jax.ShapeDtypeStruct((devices, mode_rows + PACK, wide), BF16)
    coeffs_shape = jax.ShapeDtypeStruct((groups * mode_rows, AG * channels), F32)
    p1 = pltpu.VMEM((cells_y * PITCH, wide), F32)
    sums = pltpu.VMEM((K * PITCH, wide), F32)
    weight = spectral_weight.reshape(groups, AG, mode_rows, channels * channels)

    def exchange(values_in):
        return lax.all_to_all(values_in, "gx", 0, 0, tiled=True)

    def in_hbm(array):
        return pltpu.with_memory_space_constraint(array, pltpu.HBM)

    projected = pl.pallas_call(
        functools.partial(project_kernel, chunks=chunks, cells_y=cells_y),
        grid=(steps,),
        in_specs=[field_spec, whole(table["z"]), whole(table["y"])],
        out_specs=whole(blocks),
        out_shape=blocks,
        scratch_shapes=[p1, sums],
        compiler_params=params(16),
        name="project",
    )(in_hbm(state_field), in_hbm(table["z"]), in_hbm(table["y"]))
    got = exchange(projected)
    mixed, coeffs = pl.pallas_call(
        mix_kernel,
        in_specs=[in_vmem] * 5,
        out_specs=[in_vmem] * 2,
        out_shape=[blocks, coeffs_shape],
        compiler_params=params(16),
        name="mix",
    )(got, weight, table["x"], table["sel_c"], table["fold_c"])
    got = exchange(mixed)
    bias_row = local_bias.reshape(1, channels)
    layer_output, hidden, projected = pl.pallas_call(
        functools.partial(layer_kernel, chunks=chunks, cells_y=cells_y),
        grid=(steps,),
        in_specs=[in_vmem] * 10,
        out_specs=[field_spec, in_vmem, in_vmem],
        out_shape=[
            jax.ShapeDtypeStruct(state_field.shape, BF16),
            jax.ShapeDtypeStruct((wide, cells), BF16),
            packed,
        ],
        scratch_shapes=[
            p1, p1, sums, pltpu.VMEM((wide, wide), BF16),
            pltpu.VMEM((wide, 128), F32), pltpu.VMEM((wide + 16, wide), F32),
        ],
        compiler_params=params(16),
        name="layer",
    )(
        got, state_field, cotangent, local_weight, bias_row,
        table["z"], table["y"], table["yt"], table["eye"], table["rep"],
    )
    got = exchange(projected)
    back, grads, local = pl.pallas_call(
        back_kernel,
        in_specs=[in_vmem] * 5,
        out_specs=[in_vmem] * 3,
        out_shape=[blocks, coeffs_shape, jax.ShapeDtypeStruct((2, channels, channels), F32)],
        compiler_params=params(16),
        name="back",
    )(got, weight, table["x"], table["sel_o"], table["fold_o"])
    got = exchange(back)
    pairs = channels * channels
    spectral_grad = pl.pallas_call(
        spectral_kernel,
        grid=(AG,),
        in_specs=[
            in_vmem, in_vmem,
            pl.BlockSpec((1,) + table["sel_c"].shape[1:], lambda i: (i, 0, 0)),
            pl.BlockSpec((1,) + table["sel_o"].shape[1:], lambda i: (i, 0, 0)),
        ],
        out_specs=pl.BlockSpec((groups, 1, mode_rows, pairs), lambda i: (0, i, 0, 0)),
        out_shape=jax.ShapeDtypeStruct((groups, AG, mode_rows, pairs), F32),
        compiler_params=params(16),
        cost_estimate=pl.CostEstimate(
            flops=2 * 256 * K * mode_rows * pairs, bytes_accessed=4 * K * mode_rows * pairs, transcendentals=0
        ),
        name="spectral",
    )(coeffs, grads, table["sel_c"], table["sel_o"])
    field_grad = pl.pallas_call(
        functools.partial(field_grad_kernel, chunks=chunks, cells_y=cells_y),
        grid=(steps,),
        in_specs=[in_vmem] * 7,
        out_specs=field_spec,
        out_shape=jax.ShapeDtypeStruct(state_field.shape, BF16),
        scratch_shapes=[p1, sums, pltpu.VMEM((wide, wide), BF16)],
        compiler_params=params(16),
        name="field_grad",
    )(got, hidden, local_weight, table["z"], table["yt"], table["eye"], table["rep"])
    spectral_grad = spectral_grad.reshape(K, mode_rows, pairs)
    return (layer_output, field_grad, spectral_grad, local[0], local[1, 0])


def solution(mesh):
    placed = (P(None, "gx", "grp"), P(None, "gx", "grp"), P(None, "gx", None), P(), P())
    return jax.shard_map(
        body,
        mesh=mesh,
        in_specs=placed,
        out_specs=(
            P(None, "gx", "grp"),
            P(None, "gx", "grp"),
            P("grp", "gx", None),
            P("grp", None),
            P("grp"),
        ),
        check_vma=False,
    )
```

```python
import functools
import math

import jax
import jax.numpy as jnp
import numpy as np
from jax import lax
from jax.experimental import pallas as pl
from jax.experimental.pallas import tpu as pltpu
from jax.sharding import PartitionSpec as P

MODES = 16
K = 2 * MODES
NZ = 64
YC = 4
CHUNK = YC * NZ
AG = 4
PITCH = K + 1
PACK = 32
F32 = jnp.float32
BF16 = jnp.bfloat16
NN = (((1,), (0,)), ((), ()))
NT = (((1,), (1,)), ((), ()))


def dot(lhs, rhs, dims=NN, precision=None):
    return lax.dot_general(lhs, rhs, dims, precision=precision, preferred_element_type=F32)


def basis_table(length):
    cells = np.arange(length)
    rows = np.arange(K)
    frequency = np.where(rows < MODES, rows, rows - MODES + 1)
    phase_index = frequency[:, None] * cells[None, :] % length
    angles = phase_index.astype(np.float32) * np.float32(2.0 * math.pi / length)
    angles = angles.astype(np.float64)
    table = np.where((rows < MODES)[:, None], np.cos(angles), np.sin(angles))
    return (table * math.sqrt(2.0 / length)).astype(np.float32)


def halves(table):
    high = table.astype(BF16)
    low = (table - high.astype(np.float32)).astype(BF16)
    return high, low


def tables(channels, rows_x, devices, cells_y):
    table_x = basis_table(rows_x * devices)
    y_high, y_low = halves(basis_table(cells_y))
    z = basis_table(NZ).astype(BF16).astype(np.float32)
    eye_c = np.eye(channels, dtype=np.float32)
    out = {}
    out["z"] = np.kron(np.eye(YC, dtype=np.float32), z).astype(BF16)
    out["y"] = np.concatenate([y_high, y_low], 0)
    out["yt"] = np.concatenate([y_high.T, y_low.T], 1)
    out["rep"] = np.kron(eye_c, np.ones((rows_x, 1), np.float32)).astype(BF16)
    kx = table_x.reshape(K, devices, rows_x)
    kx = np.einsum("adx,ce->acdex", kx, eye_c)
    out["x"] = kx.reshape(K * channels, devices * channels * rows_x).astype(BF16)
    out["x_back"] = np.concatenate([out["x"], np.zeros_like(out["x"][:16])], 0)
    return {name: jnp.asarray(value) for name, value in out.items()}


def split(values_in):
    high = values_in.astype(BF16)
    low = (values_in - high.astype(F32)).astype(BF16)
    return jnp.concatenate([high, low], 1)


def put_chunk(ref, index, values_in):
    for i in range(YC):
        ref[pl.ds((index * YC + i) * PITCH, K), :] = values_in[i * K : (i + 1) * K]


def take_chunk(ref, index):
    parts = [ref[pl.ds((index * YC + i) * PITCH, K), :] for i in range(YC)]
    return jnp.concatenate(parts, 0).astype(BF16)


def contract_y(p1_ref, y_ref, sums_ref, cells_y):
    y = y_ref[...]
    width = p1_ref.shape[1]
    for g in range(0, K, 2):
        pair = [p1_ref[pl.ds(g + i, cells_y, stride=PITCH), :].astype(BF16) for i in range(2)]
        both = dot(y, jnp.concatenate(pair, 1))
        both = both[:K] + both[K:]
        for i in range(2):
            sums_ref[pl.ds(g + i, K, stride=PITCH), :] = both[:, i * width : (i + 1) * width]


def block_of(sums_ref, index, mode_rows):
    first = index * (mode_rows // K)
    parts = [sums_ref[(first + i) * PITCH : (first + i) * PITCH + K, :] for i in range(mode_rows // K)]
    return jnp.concatenate(parts, 0).astype(BF16)


def expand_y(got_ref, yt_ref, sums_ref, e2_ref, cells_y):
    devices, mode_rows, width = got_ref.shape
    for d in range(devices):
        block = got_ref[d].astype(F32)
        for i in range(mode_rows // K):
            first = (d * (mode_rows // K) + i) * PITCH
            sums_ref[first : first + K, :] = block[i * K : (i + 1) * K]
    yt = yt_ref[...]
    for g in range(0, K, 2):
        pair = [sums_ref[pl.ds(g + i, K, stride=PITCH), :].astype(BF16) for i in range(2)]
        rhs = jnp.concatenate(pair, 1)
        both = dot(yt, jnp.concatenate([rhs, rhs], 0))
        for i in range(2):
            e2_ref[pl.ds(g + i, cells_y, stride=PITCH), :] = both[:, i * width : (i + 1) * width]


def spread_weight(rep_ref, weight):
    rep = rep_ref[...]
    wide = dot(dot(rep, weight).astype(BF16), rep, NT)
    rows_x = rep.shape[0] // rep.shape[1]
    row = lax.broadcasted_iota(jnp.int32, wide.shape, 0)
    col = lax.broadcasted_iota(jnp.int32, wide.shape, 1)
    return jnp.where(row % rows_x == col % rows_x, wide, 0.0).astype(BF16)


def project_kernel(
    state_ref, z_any, y_any, out_ref, flat_ref, z_ref, y_ref, held_ref, p1_ref, sums_ref, sems, *, pieces, cells_y
):
    lanes = state_ref.shape[2] // pieces
    copies = [
        pltpu.make_async_copy(
            state_ref.at[:, :, i * lanes : (i + 1) * lanes], held_ref.at[:, :, i * lanes : (i + 1) * lanes], sems.at[i]
        )
        for i in range(pieces)
    ]
    copies.append(pltpu.make_async_copy(z_any, z_ref, sems.at[pieces]))
    copies.append(pltpu.make_async_copy(y_any, y_ref, sems.at[pieces + 1]))
    for i in (pieces, *range(pieces), pieces + 1):
        copies[i].start()
    copies[pieces].wait()
    z = z_ref[...]
    for j in range(state_ref.shape[2] // CHUNK):
        if j * CHUNK % lanes == 0:
            copies[j * CHUNK // lanes].wait()
        own = slice(j * CHUNK, (j + 1) * CHUNK)
        cells = held_ref[:, :, own].reshape(-1, CHUNK)
        flat_ref[:, own] = cells
        put_chunk(p1_ref, j, dot(z, cells, NT))
    copies[pieces + 1].wait()
    contract_y(p1_ref, y_ref, sums_ref, cells_y)
    devices, mode_rows, _ = out_ref.shape
    for d in range(devices):
        out_ref[d] = block_of(sums_ref, d, mode_rows)


def sum_x(got_ref, x_ref, coeffs_ref, mode_rows):
    devices, _, width = got_ref.shape
    flat = jnp.concatenate([got_ref[d, :mode_rows] for d in range(devices)], 1)
    coeffs = dot(flat, x_ref[: K * width // AG], NT)
    for t in range(K // AG):
        coeffs_ref[t * mode_rows : (t + 1) * mode_rows, :] = coeffs[:, t * width : (t + 1) * width]


def spread_x(modes, x_ref, send_ref):
    devices, mode_rows, width = send_ref.shape
    flat = jnp.concatenate([modes[t * mode_rows : (t + 1) * mode_rows] for t in range(K // AG)], 1)
    values = dot(flat, x_ref[: K * width // AG])
    for d in range(devices):
        send_ref[d] = values[:, d * width : (d + 1) * width].astype(BF16)


def ones_where(shape, test):
    row = lax.broadcasted_iota(jnp.int32, shape, 0)
    col = lax.broadcasted_iota(jnp.int32, shape, 1)
    return jnp.where(test(row, col), 1.0, 0.0).astype(BF16)


def only(values_in, a, channels):
    lane = lax.broadcasted_iota(jnp.int32, values_in.shape, 1)
    return jnp.where(lane // channels % AG == a, values_in, jnp.zeros_like(values_in))


def fetch_weight(weight_any, weight_ref, sems):
    copies = [pltpu.make_async_copy(weight_any.at[:, a], weight_ref.at[a], sems.at[a]) for a in range(AG)]
    for copy in copies:
        copy.start()
    return copies


def mix_kernel(got_ref, weight_any, x_ref, send_ref, coeffs_ref, weight_ref, sems):
    copies = fetch_weight(weight_any, weight_ref, sems)
    mode_rows, pairs = weight_ref.shape[2:]
    rows, wide = coeffs_ref.shape
    channels = wide // AG
    sum_x(got_ref, x_ref, coeffs_ref, mode_rows)
    left = split(coeffs_ref[...])
    spread_c = ones_where((2 * wide, pairs), lambda i, j: i % channels == j // channels)
    parts = []
    for a in range(AG):
        own = only(left, a, channels)
        total = None
        copies[a].wait()
        for q in range(0, pairs, 256):
            weight = weight_ref[a, :, :, q : q + 256].reshape(rows, 256).astype(F32)
            product = dot(own, spread_c[:, q : q + 256]) * weight
            product = product[:, :128] + product[:, 128:]
            total = product if total is None else total + product
        parts.append(split(total))
    fold = ones_where((AG * 256, wide), lambda i, j: (i // 256 == j // channels) & (i % channels == j % channels))
    mixed = dot(jnp.concatenate(parts, 1), fold).astype(BF16)
    spread_x(mixed, x_ref, send_ref)


def spread_o(grads, a, channels):
    pick = ones_where((grads.shape[1], 128), lambda i, j: i % channels == j % channels)
    wide = dot(only(grads, a, channels), pick)
    return jnp.concatenate([wide, wide], 1)


def back_kernel(got_ref, weight_ref, x_ref, send_ref, grads_ref, local_ref):
    mode_rows, pairs = weight_ref.shape[2:]
    rows, wide = grads_ref.shape
    channels = wide // AG
    sum_x(got_ref, x_ref, grads_ref, mode_rows)
    left = split(grads_ref[...])
    fold = ones_where((pairs, wide), lambda i, j: i // channels == j % channels)
    back = None
    for a in range(AG):
        grads = spread_o(left, a, channels)
        products = []
        for q in range(0, pairs, 256):
            weight = weight_ref[:, a, :, q : q + 256].reshape(rows, 256).astype(F32)
            products.append((grads * weight).astype(BF16))
        part = only(dot(jnp.concatenate(products, 1), fold), a, channels)
        back = part if back is None else back + part
    spread_x(back.astype(BF16), x_ref, send_ref)
    local = got_ref[0, mode_rows:].astype(F32)
    for d in range(1, got_ref.shape[0]):
        local = local + got_ref[d, mode_rows:].astype(F32)
    local_ref[0] = local[:, :channels] + local[:, channels : 2 * channels]
    local_ref[1] = local[:, 2 * channels : 3 * channels] + local[:, 3 * channels :]


def spectral_kernel(coeffs_ref, grads_ref, out_ref):
    a = pl.program_id(0)
    groups, _, mode_rows, pairs = out_ref.shape
    wide = coeffs_ref.shape[1]
    channels = wide // AG
    coeffs = only(split(coeffs_ref[...]), a, channels)
    grads = spread_o(split(grads_ref[...]), a, channels)
    spread_c = ones_where((2 * wide, pairs), lambda i, j: i % channels == j // channels)
    for q in range(0, pairs, 256):
        product = dot(coeffs, spread_c[:, q : q + 256]) * grads
        out_ref[:, 0, :, q : q + 256] = product.reshape(groups, mode_rows, 256)


GELU_A = math.sqrt(2.0 / math.pi)
GELU_B = GELU_A * 0.044715


def staged(count, stages):
    held = {}
    for tick in range(count + len(stages) - 1):
        for index, stage in enumerate(stages):
            item = tick - index
            if 0 <= item < count:
                held[item] = stage(item, held.get(item))


def layer_kernel(
    got_ref, flat_ref, cotangent_ref, weight_ref, bias_ref, z_ref, y_ref, yt_ref, rep_ref,
    output_ref, hidden_any, send_ref, held_ref, hidden_ref, e2_ref, p1_ref, sums_ref, sems, *, pieces, cells_y,
):
    rows = z_ref.shape[0]
    width = rep_ref.shape[0]
    rows_x = cotangent_ref.shape[1]
    lanes = flat_ref.shape[1] // pieces
    expand_y(got_ref, yt_ref, sums_ref, e2_ref, cells_y)
    mix = spread_weight(rep_ref, weight_ref[...].astype(F32).T.astype(BF16))
    bias = jnp.sum(rep_ref[...].astype(F32) * bias_ref[...], axis=1, keepdims=True)
    bias = jnp.broadcast_to(bias, (width, CHUNK))
    z = z_ref[...]
    ones = jnp.ones((16, CHUNK), BF16)
    total = []
    copies = []

    def turn(j, _):
        return take_chunk(e2_ref, j).T

    def evaluate(j, e2):
        left = jnp.concatenate([e2, mix], 1)
        return dot(left, jnp.concatenate([z, flat_ref[:, j * CHUNK : (j + 1) * CHUNK]], 0)) + bias

    def activate(j, pre):
        square = pre * pre
        half = 0.5 * jnp.tanh(pre * (GELU_A + GELU_B * square)) + 0.5
        own = slice(j * CHUNK, (j + 1) * CHUNK)
        held_ref[:, :, own] = (pre * half).astype(BF16).reshape(-1, rows_x, CHUNK)
        slope = half + (half - half * half) * (pre * (2 * GELU_A + 6 * GELU_B * square))
        cot = cotangent_ref[:, :, own].reshape(-1, CHUNK).astype(F32)
        hidden = (cot * slope).astype(BF16)
        hidden_ref[:, own] = hidden
        if (j + 1) * CHUNK % lanes == 0:
            piece = j * CHUNK // lanes
            span = slice(piece * lanes, (piece + 1) * lanes)
            pairs = [(held_ref.at[:, :, span], output_ref.at[:, :, span]), (hidden_ref.at[:, span], hidden_any.at[:, span])]
            for i, (source, target) in enumerate(pairs):
                copies.append(pltpu.make_async_copy(source, target, sems.at[i, piece]))
                copies[-1].start()
        return hidden

    def reduce(j, hidden):
        cells = flat_ref[:, j * CHUNK : (j + 1) * CHUNK]
        sums = dot(jnp.concatenate([z, cells, ones], 0), hidden, NT)
        put_chunk(p1_ref, j, sums[:rows])
        total[:] = [total[0] + sums[rows:] if total else sums[rows:]]

    staged(flat_ref.shape[1] // CHUNK, [turn, evaluate, activate, reduce])
    contract_y(p1_ref, y_ref, sums_ref, cells_y)
    full = total[0][:width]
    row = lax.broadcasted_iota(jnp.int32, full.shape, 0)
    col = lax.broadcasted_iota(jnp.int32, full.shape, 1)
    full = jnp.where(row % rows_x == col % rows_x, full, 0.0)
    rep = rep_ref[...].astype(F32)
    high = lax.Precision.HIGHEST
    tall = dot(jnp.concatenate([full, total[0][width : width + 8]], 0), rep, precision=high)
    channels = rep.shape[1]
    local = dot(rep.T, tall[:width], precision=high)
    bias_sum = jnp.broadcast_to(tall[width : width + 1], (channels, channels))
    packed = jnp.concatenate([split(local), split(bias_sum)], 1)
    devices = send_ref.shape[0]
    mode_rows = K * K // devices
    for d in range(devices):
        send_ref[d, :mode_rows] = block_of(sums_ref, d, mode_rows)
        send_ref[d, mode_rows:] = packed
    for copy in copies:
        copy.wait()


def field_grad_kernel(
    got_ref, hidden_any, weight_ref, z_ref, yt_ref, rep_ref, output_ref, hidden_ref, held_ref, e2_ref, sums_ref, sems,
    *, pieces, cells_y,
):
    rows_x = held_ref.shape[1]
    lanes = hidden_ref.shape[1] // pieces
    arrivals = []
    for i in range(pieces):
        span = slice(i * lanes, (i + 1) * lanes)
        arrivals.append(pltpu.make_async_copy(hidden_any.at[:, span], hidden_ref.at[:, span], sems.at[1, i]))
        arrivals[-1].start()
    expand_y(got_ref, yt_ref, sums_ref, e2_ref, cells_y)
    mix = spread_weight(rep_ref, weight_ref[...])
    z = z_ref[...]
    copies = []

    def turn(j, _):
        return take_chunk(e2_ref, j).T

    def evaluate(j, e2):
        left = jnp.concatenate([e2, mix], 1)
        own = slice(j * CHUNK, (j + 1) * CHUNK)
        if j * CHUNK % lanes == 0:
            arrivals[j * CHUNK // lanes].wait()
        grad = dot(left, jnp.concatenate([z, hidden_ref[:, own]], 0))
        held_ref[:, :, own] = grad.astype(BF16).reshape(-1, rows_x, CHUNK)
        if (j + 1) * CHUNK % lanes == 0:
            piece = j * CHUNK // lanes
            span = slice(piece * lanes, (piece + 1) * lanes)
            copies.append(pltpu.make_async_copy(held_ref.at[:, :, span], output_ref.at[:, :, span], sems.at[0, piece]))
            copies[-1].start()

    staged(hidden_ref.shape[1] // CHUNK, [turn, evaluate])
    for copy in copies:
        copy.wait()


def body(state_field, cotangent, spectral_weight, local_weight, local_bias):
    channels, rows_x, cells = state_field.shape
    cells_y = cells // NZ
    devices = lax.axis_size("gx")
    mode_rows = spectral_weight.shape[1]
    wide = channels * rows_x
    groups = K // AG
    table = tables(channels, rows_x, devices, cells_y)
    pieces = 8
    in_vmem = pl.BlockSpec(memory_space=pltpu.VMEM)

    def params(mib):
        return pltpu.CompilerParams(vmem_limit_bytes=mib * 1024 * 1024)

    in_any = pl.BlockSpec(memory_space=pl.ANY)
    held = pltpu.VMEM((channels, rows_x, cells), BF16)
    sems = pltpu.SemaphoreType.DMA((2, pieces))
    flat_held = pltpu.VMEM((wide, cells), BF16)
    field = jax.ShapeDtypeStruct(state_field.shape, BF16)
    flat_field = jax.ShapeDtypeStruct((wide, cells), BF16)

    def cost(moved):
        return pl.CostEstimate(flops=0, bytes_accessed=moved, transcendentals=0)

    blocks = jax.ShapeDtypeStruct((devices, mode_rows, wide), BF16)
    packed = jax.ShapeDtypeStruct((devices, mode_rows + PACK, wide), BF16)
    coeffs_shape = jax.ShapeDtypeStruct((groups * mode_rows, AG * channels), F32)
    p1 = pltpu.VMEM((cells_y * PITCH, wide), F32)
    sums = pltpu.VMEM((K * PITCH, wide), F32)
    weight = spectral_weight.reshape(groups, AG, mode_rows, channels * channels)
    weight_scratch = [
        pltpu.VMEM((AG, groups, mode_rows, channels * channels), BF16), pltpu.SemaphoreType.DMA((AG,))
    ]

    def exchange(values_in):
        return lax.all_to_all(values_in, "gx", 0, 0, tiled=True)

    def in_hbm(array):
        return pltpu.with_memory_space_constraint(array, pltpu.HBM)

    projected, flat = pl.pallas_call(
        functools.partial(project_kernel, pieces=pieces, cells_y=cells_y),
        in_specs=[in_any] * 3,
        out_specs=[in_vmem, in_vmem],
        out_shape=[blocks, flat_field],
        scratch_shapes=[
            pltpu.VMEM(table["z"].shape, BF16), pltpu.VMEM(table["y"].shape, BF16),
            held, p1, sums, pltpu.SemaphoreType.DMA((pieces + 2,)),
        ],
        compiler_params=params(12),
        cost_estimate=cost(48 << 20),
        name="project",
    )(in_hbm(state_field), in_hbm(table["z"]), in_hbm(table["y"]))
    got = exchange(projected)
    mixed, coeffs = pl.pallas_call(
        mix_kernel,
        in_specs=[in_vmem, in_any, in_vmem],
        out_specs=[in_vmem] * 2,
        out_shape=[blocks, coeffs_shape],
        scratch_shapes=weight_scratch,
        compiler_params=params(14),
        cost_estimate=cost(48 << 20),
        name="mix",
    )(got, in_hbm(weight), table["x"])
    got = exchange(mixed)
    bias_row = local_bias.reshape(1, channels)
    layer_output, hidden, projected = pl.pallas_call(
        functools.partial(layer_kernel, pieces=pieces, cells_y=cells_y),
        in_specs=[in_vmem] * 9,
        out_specs=[in_any, in_any, in_vmem],
        out_shape=[field, flat_field, packed],
        scratch_shapes=[held, flat_held, p1, p1, sums, sems],
        compiler_params=params(26),
        cost_estimate=cost(64 << 20),
        name="layer",
    )(
        got, flat, cotangent, local_weight, bias_row,
        table["z"], table["y"], table["yt"], table["rep"],
    )
    got = exchange(projected)
    back, grads, local = pl.pallas_call(
        back_kernel,
        in_specs=[in_vmem] * 3,
        out_specs=[in_vmem] * 3,
        out_shape=[blocks, coeffs_shape, jax.ShapeDtypeStruct((2, channels, channels), F32)],
        compiler_params=params(10),
        cost_estimate=cost(48 << 20),
        name="back",
    )(got, weight, table["x_back"])
    got = exchange(back)
    pairs = channels * channels
    spectral_grad = pl.pallas_call(
        spectral_kernel,
        grid=(AG,),
        in_specs=[in_vmem] * 2,
        out_specs=pl.BlockSpec((groups, 1, mode_rows, pairs), lambda i: (0, i, 0, 0)),
        out_shape=jax.ShapeDtypeStruct((groups, AG, mode_rows, pairs), F32),
        compiler_params=params(10),
        cost_estimate=pl.CostEstimate(
            flops=2 * 256 * K * mode_rows * pairs, bytes_accessed=4 * K * mode_rows * pairs, transcendentals=0
        ),
        name="spectral",
    )(coeffs, grads)
    field_grad = pl.pallas_call(
        functools.partial(field_grad_kernel, pieces=pieces, cells_y=cells_y),
        in_specs=[in_vmem, in_any] + [in_vmem] * 4,
        out_specs=in_any,
        out_shape=field,
        scratch_shapes=[flat_held, held, p1, sums, sems],
        compiler_params=params(16),
        cost_estimate=cost(48 << 20),
        name="field_grad",
    )(got, in_hbm(hidden), local_weight, table["z"], table["yt"], table["rep"])
    spectral_grad = spectral_grad.reshape(K, mode_rows, pairs)
    return (layer_output, field_grad, spectral_grad, local[0], local[1, 0])


def solution(mesh):
    placed = (P(None, "gx", "grp"), P(None, "gx", "grp"), P(None, "gx", None), P(), P())
    return jax.shard_map(
        body,
        mesh=mesh,
        in_specs=placed,
        out_specs=(
            P(None, "gx", "grp"),
            P(None, "gx", "grp"),
            P("grp", "gx", None),
            P("grp", None),
            P("grp"),
        ),
        check_vma=False,
    )
```

```python
import functools
import math

import jax
import jax.numpy as jnp
import numpy as np
from jax import lax
from jax.experimental import pallas as pl
from jax.experimental.pallas import tpu as pltpu
from jax.sharding import PartitionSpec as P

MODES = 16
K = 2 * MODES
NZ = 64
YC = 4
CHUNK = YC * NZ
AG = 4
PITCH = K + 1
PACK = 32
F32 = jnp.float32
BF16 = jnp.bfloat16
NN = (((1,), (0,)), ((), ()))
NT = (((1,), (1,)), ((), ()))


def dot(lhs, rhs, dims=NN, precision=None):
    return lax.dot_general(lhs, rhs, dims, precision=precision, preferred_element_type=F32)


def basis_table(length):
    cells = np.arange(length)
    rows = np.arange(K)
    frequency = np.where(rows < MODES, rows, rows - MODES + 1)
    phase_index = frequency[:, None] * cells[None, :] % length
    angles = phase_index.astype(np.float32) * np.float32(2.0 * math.pi / length)
    angles = angles.astype(np.float64)
    table = np.where((rows < MODES)[:, None], np.cos(angles), np.sin(angles))
    return (table * math.sqrt(2.0 / length)).astype(np.float32)


def halves(table):
    high = table.astype(BF16)
    low = (table - high.astype(np.float32)).astype(BF16)
    return high, low


def tables(channels, rows_x, devices, cells_y):
    table_x = basis_table(rows_x * devices)
    y_high, y_low = halves(basis_table(cells_y))
    z = basis_table(NZ).astype(BF16).astype(np.float32)
    eye_c = np.eye(channels, dtype=np.float32)
    out = {}
    out["z"] = np.kron(np.eye(YC, dtype=np.float32), z).astype(BF16)
    out["y"] = np.concatenate([y_high, y_low], 0)
    out["yt"] = np.concatenate([y_high.T, y_low.T], 1)
    out["rep"] = np.kron(eye_c, np.ones((rows_x, 1), np.float32)).astype(BF16)
    kx = table_x.reshape(K, devices, rows_x)
    kx = np.einsum("adx,ce->acdex", kx, eye_c)
    out["x"] = kx.reshape(K * channels, devices * channels * rows_x).astype(BF16)
    rows = table_x.reshape(K, devices, 1, rows_x)
    rows = np.broadcast_to(rows, (K, devices, channels, rows_x))
    out["x_rows"] = rows.reshape(K, devices * channels * rows_x).astype(BF16)
    return {name: jnp.asarray(value) for name, value in out.items()}


def split(values_in):
    high = values_in.astype(BF16)
    low = (values_in - high.astype(F32)).astype(BF16)
    return jnp.concatenate([high, low], 1)


def put_chunk(ref, base, index, values_in):
    for i in range(YC):
        ref[pl.ds(base + (index * YC + i) * PITCH, K), :] = values_in[i * K : (i + 1) * K]


def take_chunk(ref, base, index):
    parts = [ref[pl.ds(base + (index * YC + i) * PITCH, K), :] for i in range(YC)]
    return jnp.concatenate(parts, 0).astype(BF16)


def contract_y(p1_ref, y_ref, sums_ref, cells_y):
    y = y_ref[...]
    width = p1_ref.shape[1]
    for g in range(0, K, 2):
        pair = [p1_ref[pl.ds(g + i, cells_y, stride=PITCH), :].astype(BF16) for i in range(2)]
        both = dot(y, jnp.concatenate(pair, 1))
        both = both[:K] + both[K:]
        for i in range(2):
            sums_ref[pl.ds(g + i, K, stride=PITCH), :] = both[:, i * width : (i + 1) * width]


def block_of(sums_ref, index, mode_rows):
    first = index * (mode_rows // K)
    parts = [sums_ref[(first + i) * PITCH : (first + i) * PITCH + K, :] for i in range(mode_rows // K)]
    return jnp.concatenate(parts, 0).astype(BF16)


def expand_y(got_ref, yt_ref, sums_ref, e2_ref, cells_y):
    devices, mode_rows, width = got_ref.shape
    for d in range(devices):
        block = got_ref[d].astype(F32)
        for i in range(mode_rows // K):
            first = (d * (mode_rows // K) + i) * PITCH
            sums_ref[first : first + K, :] = block[i * K : (i + 1) * K]
    yt = yt_ref[...]
    for g in range(0, K, 2):
        pair = [sums_ref[pl.ds(g + i, K, stride=PITCH), :].astype(BF16) for i in range(2)]
        rhs = jnp.concatenate(pair, 1)
        both = dot(yt, jnp.concatenate([rhs, rhs], 0))
        for i in range(2):
            e2_ref[pl.ds(g + i, cells_y, stride=PITCH), :] = both[:, i * width : (i + 1) * width]


def spread_weight(rep_ref, weight):
    rep = rep_ref[...]
    wide = dot(dot(rep, weight).astype(BF16), rep, NT)
    rows_x = rep.shape[0] // rep.shape[1]
    row = lax.broadcasted_iota(jnp.int32, wide.shape, 0)
    col = lax.broadcasted_iota(jnp.int32, wide.shape, 1)
    return jnp.where(row % rows_x == col % rows_x, wide, 0.0).astype(BF16)


def project_kernel(
    state_ref, z_any, y_any, rows_any, out_ref, flat_ref, x_ref, z_ref, y_ref, rows_ref, held_ref, p1_ref, sums_ref, sems, *, pieces, loops, cells_y
):
    lanes = state_ref.shape[2] // pieces

    def piece(i):
        span = pl.ds(pl.multiple_of(i * lanes, lanes), lanes)
        return pltpu.make_async_copy(state_ref.at[:, :, span], held_ref.at[:, :, span], sems.at[i])

    copy_z = pltpu.make_async_copy(z_any, z_ref, sems.at[pieces])
    copy_y = pltpu.make_async_copy(y_any, y_ref, sems.at[pieces + 1])
    copy_rows = pltpu.make_async_copy(rows_any, rows_ref, sems.at[pieces + 2])
    copy_rows.start()
    copy_z.start()
    for i in range(pieces):
        piece(i).start()
    copy_y.start()
    copy_rows.wait()
    channels, rows_x, _ = state_ref.shape
    shape = (channels, rows_ref.shape[1])
    row = lax.broadcasted_iota(jnp.int32, shape, 0)
    col = lax.broadcasted_iota(jnp.int32, shape, 1)
    own_channel = row == col // rows_x % channels
    rows = rows_ref[...].astype(F32)
    for a in range(K):
        wide = jnp.where(own_channel, jnp.broadcast_to(rows[a : a + 1], shape), 0.0)
        x_ref[a * channels : (a + 1) * channels, :] = wide.astype(BF16)
    copy_z.wait()
    chunks = state_ref.shape[2] // CHUNK // loops
    per = pieces // loops

    for i in range(loops):
        base = i * chunks * YC * PITCH
        z = z_ref[...]
        for j in range(chunks):
            if j % (chunks // per) == 0:
                piece(i * per + j // (chunks // per)).wait()
            own = pl.ds(pl.multiple_of((i * chunks + j) * CHUNK, CHUNK), CHUNK)
            cells = held_ref[:, :, own].reshape(-1, CHUNK)
            flat_ref[:, own] = cells
            put_chunk(p1_ref, base, j, dot(z, cells, NT))

    copy_y.wait()
    contract_y(p1_ref, y_ref, sums_ref, cells_y)
    devices, mode_rows, _ = out_ref.shape
    for d in range(devices):
        out_ref[d] = block_of(sums_ref, d, mode_rows)


def sum_x(got_ref, x_ref, coeffs_ref, mode_rows):
    devices, _, width = got_ref.shape
    flat = jnp.concatenate([got_ref[d, :mode_rows] for d in range(devices)], 1)
    coeffs = dot(flat, x_ref[...], NT)
    for t in range(K // AG):
        coeffs_ref[t * mode_rows : (t + 1) * mode_rows, :] = coeffs[:, t * width : (t + 1) * width]


def spread_x(modes, x_ref, send_ref):
    devices, mode_rows, width = send_ref.shape
    flat = jnp.concatenate([modes[t * mode_rows : (t + 1) * mode_rows] for t in range(K // AG)], 1)
    values = dot(flat, x_ref[...])
    for d in range(devices):
        send_ref[d] = values[:, d * width : (d + 1) * width].astype(BF16)


def ones_where(shape, test):
    row = lax.broadcasted_iota(jnp.int32, shape, 0)
    col = lax.broadcasted_iota(jnp.int32, shape, 1)
    return jnp.where(test(row, col), 1.0, 0.0).astype(BF16)


def only(values_in, a, channels):
    lane = lax.broadcasted_iota(jnp.int32, values_in.shape, 1)
    return jnp.where(lane // channels % AG == a, values_in, jnp.zeros_like(values_in))


def mix_kernel(got_ref, weight_ref, x_ref, send_ref, coeffs_ref):
    mode_rows, pairs = weight_ref.shape[2:]
    rows, wide = coeffs_ref.shape
    channels = wide // AG
    sum_x(got_ref, x_ref, coeffs_ref, mode_rows)
    left = split(coeffs_ref[...])
    spread_c = ones_where((2 * wide, pairs), lambda i, j: i % channels == j // channels)
    parts = []
    for a in range(AG):
        own = only(left, a, channels)
        total = None
        for q in range(0, pairs, 256):
            weight = weight_ref[:, a, :, q : q + 256].reshape(rows, 256).astype(F32)
            product = dot(own, spread_c[:, q : q + 256]) * weight
            product = product[:, :128] + product[:, 128:]
            total = product if total is None else total + product
        parts.append(split(total))
    fold = ones_where((AG * 256, wide), lambda i, j: (i // 256 == j // channels) & (i % channels == j % channels))
    mixed = dot(jnp.concatenate(parts, 1), fold).astype(BF16)
    spread_x(mixed, x_ref, send_ref)


def spread_o(grads, a, channels):
    pick = ones_where((grads.shape[1], 128), lambda i, j: i % channels == j % channels)
    wide = dot(only(grads, a, channels), pick)
    return jnp.concatenate([wide, wide], 1)


def back_kernel(got_ref, weight_ref, x_ref, send_ref, grads_ref, local_ref, bias_ref):
    mode_rows, pairs = weight_ref.shape[2:]
    rows, wide = grads_ref.shape
    channels = wide // AG
    sum_x(got_ref, x_ref, grads_ref, mode_rows)
    left = split(grads_ref[...])
    fold = ones_where((pairs, wide), lambda i, j: i // channels == j % channels)
    back = None
    for a in range(AG):
        grads = spread_o(left, a, channels)
        products = []
        for q in range(0, pairs, 256):
            weight = weight_ref[:, a, :, q : q + 256].reshape(rows, 256).astype(F32)
            products.append((grads * weight).astype(BF16))
        part = only(dot(jnp.concatenate(products, 1), fold), a, channels)
        back = part if back is None else back + part
    spread_x(back.astype(BF16), x_ref, send_ref)
    local = got_ref[0, mode_rows:].astype(F32)
    for d in range(1, got_ref.shape[0]):
        local = local + got_ref[d, mode_rows:].astype(F32)
    local_ref[...] = local[:, :channels] + local[:, channels : 2 * channels]
    bias_ref[...] = local[:1, 2 * channels : 3 * channels] + local[:1, 3 * channels :]


def spectral_kernel(coeffs_ref, grads_ref, out_ref):
    a = pl.program_id(0)
    groups, _, mode_rows, pairs = out_ref.shape
    wide = coeffs_ref.shape[1]
    channels = wide // AG
    coeffs = only(split(coeffs_ref[...]), a, channels)
    grads = spread_o(split(grads_ref[...]), a, channels)
    spread_c = ones_where((2 * wide, pairs), lambda i, j: i % channels == j // channels)
    for q in range(0, pairs, 256):
        product = dot(coeffs, spread_c[:, q : q + 256]) * grads
        out_ref[:, 0, :, q : q + 256] = product.reshape(groups, mode_rows, 256)


GELU_A = math.sqrt(2.0 / math.pi)
GELU_B = GELU_A * 0.044715


def staged(count, stages):
    held = {}
    for tick in range(count + len(stages) - 1):
        for index, stage in enumerate(stages):
            item = tick - index
            if 0 <= item < count:
                held[item] = stage(item, held.get(item))


def layer_kernel(
    got_ref, flat_ref, cotangent_ref, weight_ref, bias_ref, z_ref, y_ref, yt_ref, rep_ref,
    output_ref, hidden_ref, send_ref, held_ref, e2_ref, p1_ref, sums_ref, sems, *, pieces, loops, cells_y,
):
    rows = z_ref.shape[0]
    width = rep_ref.shape[0]
    rows_x = cotangent_ref.shape[1]
    lanes = flat_ref.shape[1] // pieces
    expand_y(got_ref, yt_ref, sums_ref, e2_ref, cells_y)
    mix = spread_weight(rep_ref, weight_ref[...].astype(F32).T.astype(BF16))
    bias = jnp.sum(rep_ref[...].astype(F32) * bias_ref[...], axis=1, keepdims=True)
    bias = jnp.broadcast_to(bias, (width, CHUNK))
    ones = jnp.ones((16, CHUNK), BF16)
    chunks = flat_ref.shape[1] // CHUNK // loops
    per = pieces // loops

    def send_piece(i):
        span = pl.ds(pl.multiple_of(i * lanes, lanes), lanes)
        return pltpu.make_async_copy(held_ref.at[:, :, span], output_ref.at[:, :, span], sems.at[0, i])

    def piece(i, total):
        base = pl.multiple_of(i * (chunks * YC * PITCH), 8)
        z = z_ref[...]
        totals = [total]

        def lanes_of(j):
            return pl.ds(pl.multiple_of((i * chunks + j) * CHUNK, CHUNK), CHUNK)

        def turn(j, _):
            return take_chunk(e2_ref, base, j).T

        def evaluate(j, e2):
            left = jnp.concatenate([e2, mix], 1)
            return dot(left, jnp.concatenate([z, flat_ref[:, lanes_of(j)]], 0)) + bias

        def activate(j, pre):
            own = lanes_of(j)
            square = pre * pre
            half = 0.5 * jnp.tanh(pre * (GELU_A + GELU_B * square)) + 0.5
            held_ref[:, :, own] = (pre * half).astype(BF16).reshape(-1, rows_x, CHUNK)
            slope = half + (half - half * half) * (pre * (2 * GELU_A + 6 * GELU_B * square))
            cot = cotangent_ref[:, :, own].reshape(-1, CHUNK).astype(F32)
            hidden = (cot * slope).astype(BF16)
            hidden_ref[:, own] = hidden
            if (j + 1) % (chunks // per) == 0:
                send_piece(i * per + j // (chunks // per)).start()
            return hidden

        def reduce(j, hidden):
            cells = flat_ref[:, lanes_of(j)]
            sums = dot(jnp.concatenate([z, cells, ones], 0), hidden, NT)
            put_chunk(p1_ref, base, j, sums[:rows])
            totals[0] = totals[0] + sums[rows:]

        staged(chunks, [turn, evaluate, activate, reduce])
        return totals[0]

    total = [lax.fori_loop(0, loops, piece, jnp.zeros((width + 16, width), F32))]
    contract_y(p1_ref, y_ref, sums_ref, cells_y)
    full = total[0][:width]
    row = lax.broadcasted_iota(jnp.int32, full.shape, 0)
    col = lax.broadcasted_iota(jnp.int32, full.shape, 1)
    full = jnp.where(row % rows_x == col % rows_x, full, 0.0)
    rep = rep_ref[...].astype(F32)
    high = lax.Precision.HIGHEST
    tall = dot(jnp.concatenate([full, total[0][width : width + 8]], 0), rep, precision=high)
    channels = rep.shape[1]
    local = dot(rep.T, tall[:width], precision=high)
    bias_sum = jnp.broadcast_to(tall[width : width + 1], (channels, channels))
    packed = jnp.concatenate([split(local), split(bias_sum)], 1)
    devices = send_ref.shape[0]
    mode_rows = K * K // devices
    for d in range(devices):
        send_ref[d, :mode_rows] = block_of(sums_ref, d, mode_rows)
        send_ref[d, mode_rows:] = packed
    for i in range(pieces):
        send_piece(i).wait()


def field_grad_kernel(
    got_ref, hidden_any, weight_ref, z_ref, yt_ref, rep_ref, output_ref, hidden_ref, held_ref, e2_ref, sums_ref, sems,
    *, pieces, loops, cells_y,
):
    rows_x = held_ref.shape[1]
    lanes = hidden_ref.shape[1] // pieces

    def span(i):
        return pl.ds(pl.multiple_of(i * lanes, lanes), lanes)

    def take_piece(i):
        return pltpu.make_async_copy(hidden_any.at[:, span(i)], hidden_ref.at[:, span(i)], sems.at[1, i])

    def send_piece(i):
        return pltpu.make_async_copy(held_ref.at[:, :, span(i)], output_ref.at[:, :, span(i)], sems.at[0, i])

    for i in range(pieces):
        take_piece(i).start()
    expand_y(got_ref, yt_ref, sums_ref, e2_ref, cells_y)
    mix = spread_weight(rep_ref, weight_ref[...])
    chunks = hidden_ref.shape[1] // CHUNK // loops
    per = pieces // loops

    for i in range(loops):
        base = i * chunks * YC * PITCH
        z = z_ref[...]

        def turn(j, _):
            return take_chunk(e2_ref, base, j).T

        def evaluate(j, e2):
            left = jnp.concatenate([e2, mix], 1)
            own = pl.ds(pl.multiple_of((i * chunks + j) * CHUNK, CHUNK), CHUNK)
            if j % (chunks // per) == 0:
                take_piece(i * per + j // (chunks // per)).wait()
            grad = dot(left, jnp.concatenate([z, hidden_ref[:, own]], 0))
            held_ref[:, :, own] = grad.astype(BF16).reshape(-1, rows_x, CHUNK)
            if (j + 1) % (chunks // per) == 0:
                send_piece(i * per + j // (chunks // per)).start()

        staged(chunks, [turn, evaluate])

    for i in range(pieces):
        send_piece(i).wait()


def body(state_field, cotangent, spectral_weight, local_weight, local_bias):
    channels, rows_x, cells = state_field.shape
    cells_y = cells // NZ
    devices = lax.axis_size("gx")
    mode_rows = spectral_weight.shape[1]
    wide = channels * rows_x
    groups = K // AG
    table = tables(channels, rows_x, devices, cells_y)
    pieces = 4
    in_vmem = pl.BlockSpec(memory_space=pltpu.VMEM)

    def params(mib):
        return pltpu.CompilerParams(vmem_limit_bytes=mib * 1024 * 1024)

    in_any = pl.BlockSpec(memory_space=pl.ANY)
    held = pltpu.VMEM((channels, rows_x, cells), BF16)
    sems = pltpu.SemaphoreType.DMA((2, pieces))
    field = jax.ShapeDtypeStruct(state_field.shape, BF16)
    flat_field = jax.ShapeDtypeStruct((wide, cells), BF16)

    def cost(moved):
        return pl.CostEstimate(flops=0, bytes_accessed=moved, transcendentals=0)

    blocks = jax.ShapeDtypeStruct((devices, mode_rows, wide), BF16)
    packed = jax.ShapeDtypeStruct((devices, mode_rows + PACK, wide), BF16)
    coeffs_shape = jax.ShapeDtypeStruct((groups * mode_rows, AG * channels), F32)
    p1 = pltpu.VMEM((cells_y * PITCH, wide), F32)
    sums = pltpu.VMEM((K * PITCH, wide), F32)
    weight = spectral_weight.reshape(groups, AG, mode_rows, channels * channels)

    def exchange(values_in):
        return lax.all_to_all(values_in, "gx", 0, 0, tiled=True)

    def in_hbm(array):
        return pltpu.with_memory_space_constraint(array, pltpu.HBM)

    projected, flat, x_table = pl.pallas_call(
        functools.partial(project_kernel, pieces=pieces, loops=1, cells_y=cells_y),
        in_specs=[in_any] * 4,
        out_specs=[in_vmem] * 3,
        out_shape=[blocks, flat_field, jax.ShapeDtypeStruct(table["x"].shape, BF16)],
        scratch_shapes=[
            pltpu.VMEM(table["z"].shape, BF16), pltpu.VMEM(table["y"].shape, BF16),
            pltpu.VMEM(table["x_rows"].shape, BF16),
            held, p1, sums, pltpu.SemaphoreType.DMA((pieces + 3,)),
        ],
        compiler_params=params(18),
        cost_estimate=cost(48 << 20),
        name="project",
    )(in_hbm(state_field), in_hbm(table["z"]), in_hbm(table["y"]), in_hbm(table["x_rows"]))
    got = exchange(projected)
    mixed, coeffs = pl.pallas_call(
        mix_kernel,
        in_specs=[in_vmem] * 3,
        out_specs=[in_vmem] * 2,
        out_shape=[blocks, coeffs_shape],
        compiler_params=params(10),
        cost_estimate=cost(48 << 20),
        name="mix",
    )(got, weight, x_table)
    got = exchange(mixed)
    bias_row = local_bias.reshape(1, channels)
    layer_output, hidden, projected = pl.pallas_call(
        functools.partial(layer_kernel, pieces=pieces, loops=2, cells_y=cells_y),
        in_specs=[in_vmem] * 9,
        out_specs=[in_any, in_vmem, in_vmem],
        out_shape=[field, flat_field, packed],
        scratch_shapes=[held, p1, p1, sums, sems],
        compiler_params=params(22),
        cost_estimate=cost(64 << 20),
        name="layer",
    )(
        got, flat, cotangent, local_weight, bias_row,
        table["z"], table["y"], table["yt"], table["rep"],
    )
    got = exchange(projected)
    back, grads, local, bias_grad = pl.pallas_call(
        back_kernel,
        in_specs=[in_vmem] * 3,
        out_specs=[in_vmem] * 4,
        out_shape=[
            blocks, coeffs_shape,
            jax.ShapeDtypeStruct((channels, channels), F32), jax.ShapeDtypeStruct((1, channels), F32),
        ],
        compiler_params=params(10),
        cost_estimate=cost(48 << 20),
        name="back",
    )(got, weight, table["x"])
    got = exchange(back)
    pairs = channels * channels
    spectral_grad = pl.pallas_call(
        spectral_kernel,
        grid=(AG,),
        in_specs=[in_vmem, in_vmem],
        out_specs=pl.BlockSpec((groups, 1, mode_rows, pairs), lambda i: (0, i, 0, 0)),
        out_shape=jax.ShapeDtypeStruct((groups, AG, mode_rows, pairs), F32),
        compiler_params=params(10),
        cost_estimate=pl.CostEstimate(
            flops=2 * 256 * K * mode_rows * pairs, bytes_accessed=4 * K * mode_rows * pairs, transcendentals=0
        ),
        name="spectral",
    )(coeffs, grads)
    field_grad = pl.pallas_call(
        functools.partial(field_grad_kernel, pieces=pieces, loops=1, cells_y=cells_y),
        in_specs=[in_vmem, in_any] + [in_vmem] * 4,
        out_specs=in_any,
        out_shape=field,
        scratch_shapes=[pltpu.VMEM((wide, cells), BF16), held, p1, sums, sems],
        compiler_params=params(16),
        cost_estimate=cost(48 << 20),
        name="field_grad",
    )(got, in_hbm(hidden), local_weight, table["z"], table["yt"], table["rep"])
    spectral_grad = spectral_grad.reshape(K, mode_rows, pairs)
    return (layer_output, field_grad, spectral_grad, local, bias_grad.reshape(channels))


def solution(mesh):
    placed = (P(None, "gx", "grp"), P(None, "gx", "grp"), P(None, "gx", None), P(), P())
    return jax.shard_map(
        body,
        mesh=mesh,
        in_specs=placed,
        out_specs=(
            P(None, "gx", "grp"),
            P(None, "gx", "grp"),
            P("grp", "gx", None),
            P("grp", None),
            P("grp"),
        ),
        check_vma=False,
    )
```

```python
import functools
import math

import jax
import jax.numpy as jnp
import numpy as np
from jax import lax
from jax.experimental import pallas as pl
from jax.experimental.pallas import tpu as pltpu
from jax.sharding import PartitionSpec as P

MODES = 16
K = 2 * MODES
NZ = 64
YC = 4
CHUNK = YC * NZ
AG = 4
PIECES = 4
PITCH = K + 1
PACK = 16
F32 = jnp.float32
BF16 = jnp.bfloat16
NN = (((1,), (0,)), ((), ()))
NT = (((1,), (1,)), ((), ()))


def dot(lhs, rhs, dims=NN, precision=None):
    return lax.dot_general(lhs, rhs, dims, precision=precision, preferred_element_type=F32)


def basis_table(length):
    cells = np.arange(length)
    rows = np.arange(K)
    frequency = np.where(rows < MODES, rows, rows - MODES + 1)
    phase_index = frequency[:, None] * cells[None, :] % length
    angles = phase_index.astype(np.float32) * np.float32(2.0 * math.pi / length)
    angles = angles.astype(np.float64)
    table = np.where((rows < MODES)[:, None], np.cos(angles), np.sin(angles))
    return (table * math.sqrt(2.0 / length)).astype(np.float32)


def halves(table):
    high = table.astype(BF16)
    low = (table - high.astype(np.float32)).astype(BF16)
    return high, low


def tables(channels, rows_x, devices, cells_y):
    table_x = basis_table(rows_x * devices)
    y_high, y_low = halves(basis_table(cells_y))
    z = basis_table(NZ).astype(BF16).astype(np.float32)
    eye_c = np.eye(channels, dtype=np.float32)
    out = {}
    out["z"] = np.kron(np.eye(YC, dtype=np.float32), z).astype(BF16)
    out["y"] = np.concatenate([y_high, y_low], 0)
    out["yt"] = np.concatenate([y_high.T, y_low.T], 1)
    out["rep"] = np.kron(eye_c, np.ones((rows_x, 1), np.float32)).astype(BF16)
    kx = table_x.reshape(K, devices, rows_x)
    kx = np.einsum("adx,ce->acdex", kx, eye_c)
    out["x"] = kx.reshape(K * channels, devices * channels * rows_x).astype(BF16)
    rows = table_x.reshape(K, devices, 1, rows_x)
    rows = np.broadcast_to(rows, (K, devices, channels, rows_x))
    out["x_rows"] = rows.reshape(K, devices * channels * rows_x).astype(BF16)
    return {name: jnp.asarray(value) for name, value in out.items()}


def split(values_in):
    high = values_in.astype(BF16)
    low = (values_in - high.astype(F32)).astype(BF16)
    return jnp.concatenate([high, low], 1)


def put_chunk(ref, base, index, values_in):
    for i in range(YC):
        ref[pl.ds(base + (index * YC + i) * PITCH, K), :] = values_in[i * K : (i + 1) * K]


def take_chunk(ref, base, index):
    parts = [ref[pl.ds(base + (index * YC + i) * PITCH, K), :] for i in range(YC)]
    return jnp.concatenate(parts, 0).astype(BF16)


def contract_y(p1_ref, y_ref, sums_ref, cells_y):
    y = y_ref[...]
    width = p1_ref.shape[1]
    for g in range(0, K, 2):
        pair = [p1_ref[pl.ds(g + i, cells_y, stride=PITCH), :].astype(BF16) for i in range(2)]
        both = dot(y, jnp.concatenate(pair, 1))
        both = both[:K] + both[K:]
        for i in range(2):
            sums_ref[pl.ds(g + i, K, stride=PITCH), :] = both[:, i * width : (i + 1) * width]


def block_of(sums_ref, index, mode_rows):
    first = index * (mode_rows // K)
    parts = [sums_ref[(first + i) * PITCH : (first + i) * PITCH + K, :] for i in range(mode_rows // K)]
    return jnp.concatenate(parts, 0).astype(BF16)


def expand_y(got_ref, yt_ref, sums_ref, e2_ref, cells_y):
    devices, mode_rows, width = got_ref.shape
    for d in range(devices):
        block = got_ref[d].astype(F32)
        for i in range(mode_rows // K):
            first = (d * (mode_rows // K) + i) * PITCH
            sums_ref[first : first + K, :] = block[i * K : (i + 1) * K]
    yt = yt_ref[...]
    for g in range(0, K, 2):
        pair = [sums_ref[pl.ds(g + i, K, stride=PITCH), :].astype(BF16) for i in range(2)]
        rhs = jnp.concatenate(pair, 1)
        both = dot(yt, jnp.concatenate([rhs, rhs], 0))
        for i in range(2):
            e2_ref[pl.ds(g + i, cells_y, stride=PITCH), :] = both[:, i * width : (i + 1) * width]


def spread_weight(rep_ref, weight):
    rep = rep_ref[...]
    wide = dot(dot(rep, weight).astype(BF16), rep, NT)
    rows_x = rep.shape[0] // rep.shape[1]
    row = lax.broadcasted_iota(jnp.int32, wide.shape, 0)
    col = lax.broadcasted_iota(jnp.int32, wide.shape, 1)
    return jnp.where(row % rows_x == col % rows_x, wide, 0.0).astype(BF16)


def spans_of(pieces, cells):
    return [(i * (cells // pieces), (i + 1) * (cells // pieces)) for i in range(pieces)]


def project_kernel(
    state_ref, z_any, y_any, rows_any, out_ref, flat_ref, x_ref, z_ref, y_ref, rows_ref, held_ref, p1_ref, sums_ref, sems, *, cells_y
):
    cells = state_ref.shape[2]
    pieces = [
        pltpu.make_async_copy(state_ref.at[:, :, first:end], held_ref.at[:, :, first:end], sems.at[k])
        for k, (first, end) in enumerate(spans_of(2, cells))
    ]
    starts = {first // CHUNK: piece for (first, _), piece in zip(spans_of(2, cells), pieces, strict=True)}
    copy_z = pltpu.make_async_copy(z_any, z_ref, sems.at[2])
    copy_y = pltpu.make_async_copy(y_any, y_ref, sems.at[3])
    copy_rows = pltpu.make_async_copy(rows_any, rows_ref, sems.at[4])
    copy_rows.start()
    copy_z.start()
    for piece in pieces:
        piece.start()
    copy_y.start()
    copy_rows.wait()
    channels, rows_x, _ = state_ref.shape
    shape = (channels, rows_ref.shape[1])
    row = lax.broadcasted_iota(jnp.int32, shape, 0)
    col = lax.broadcasted_iota(jnp.int32, shape, 1)
    own_channel = row == col // rows_x % channels
    rows = rows_ref[...].astype(F32)
    for a in range(K):
        wide = jnp.where(own_channel, jnp.broadcast_to(rows[a : a + 1], shape), 0.0)
        x_ref[a * channels : (a + 1) * channels, :] = wide.astype(BF16)
    copy_z.wait()
    z = z_ref[...]
    for j in range(cells // CHUNK):
        if j in starts:
            starts[j].wait()
        own = slice(j * CHUNK, (j + 1) * CHUNK)
        block = held_ref[:, :, own].reshape(-1, CHUNK)
        flat_ref[:, own] = block
        put_chunk(p1_ref, 0, j, dot(z, block, NT))
    copy_y.wait()
    contract_y(p1_ref, y_ref, sums_ref, cells_y)
    devices, mode_rows, _ = out_ref.shape
    for d in range(devices):
        out_ref[d] = block_of(sums_ref, d, mode_rows)


def sum_x(got_ref, x_ref, coeffs_ref, mode_rows):
    devices, _, width = got_ref.shape
    flat = jnp.concatenate([got_ref[d, :mode_rows] for d in range(devices)], 1)
    coeffs = dot(flat, x_ref[...], NT)
    for t in range(K // AG):
        coeffs_ref[t * mode_rows : (t + 1) * mode_rows, :] = coeffs[:, t * width : (t + 1) * width]


def spread_x(modes, x_ref, send_ref):
    devices, mode_rows, width = send_ref.shape
    flat = jnp.concatenate([modes[t * mode_rows : (t + 1) * mode_rows] for t in range(K // AG)], 1)
    values = dot(flat, x_ref[...])
    for d in range(devices):
        send_ref[d] = values[:, d * width : (d + 1) * width].astype(BF16)


def ones_where(shape, test):
    row = lax.broadcasted_iota(jnp.int32, shape, 0)
    col = lax.broadcasted_iota(jnp.int32, shape, 1)
    return jnp.where(test(row, col), 1.0, 0.0).astype(BF16)


def only(values_in, a, channels):
    lane = lax.broadcasted_iota(jnp.int32, values_in.shape, 1)
    return jnp.where(lane // channels % AG == a, values_in, jnp.zeros_like(values_in))


def mix_kernel(got_ref, weight_ref, x_ref, send_ref, coeffs_ref):
    mode_rows, pairs = weight_ref.shape[2:]
    rows, wide = coeffs_ref.shape
    channels = wide // AG
    sum_x(got_ref, x_ref, coeffs_ref, mode_rows)
    left = split(coeffs_ref[...])
    spread_c = ones_where((2 * wide, pairs), lambda i, j: i % channels == j // channels)
    parts = []
    for a in range(AG):
        own = only(left, a, channels)
        total = None
        for q in range(0, pairs, 256):
            weight = weight_ref[:, a, :, q : q + 256].reshape(rows, 256).astype(F32)
            product = dot(own, spread_c[:, q : q + 256]) * weight
            product = product[:, :128] + product[:, 128:]
            total = product if total is None else total + product
        parts.append(split(total))
    fold = ones_where((AG * 256, wide), lambda i, j: (i // 256 == j // channels) & (i % channels == j % channels))
    mixed = dot(jnp.concatenate(parts, 1), fold).astype(BF16)
    spread_x(mixed, x_ref, send_ref)


def spread_o(grads, a, channels):
    pick = ones_where((grads.shape[1], 128), lambda i, j: i % channels == j % channels)
    wide = dot(only(grads, a, channels), pick)
    return jnp.concatenate([wide, wide], 1)


def back_kernel(got_ref, weight_ref, x_ref, send_ref, grads_ref, local_ref, bias_ref):
    mode_rows, pairs = weight_ref.shape[2:]
    rows, wide = grads_ref.shape
    channels = wide // AG
    sum_x(got_ref, x_ref, grads_ref, mode_rows)
    left = split(grads_ref[...])
    fold = ones_where((pairs, wide), lambda i, j: i // channels == j % channels)
    back = None
    for a in range(AG):
        grads = spread_o(left, a, channels)
        products = []
        for q in range(0, pairs, 256):
            weight = weight_ref[:, a, :, q : q + 256].reshape(rows, 256).astype(F32)
            products.append((grads * weight).astype(BF16))
        part = only(dot(jnp.concatenate(products, 1), fold), a, channels)
        back = part if back is None else back + part
    spread_x(back.astype(BF16), x_ref, send_ref)
    local = got_ref[0, mode_rows:].astype(F32)
    for d in range(1, got_ref.shape[0]):
        local = local + got_ref[d, mode_rows:].astype(F32)
    for i in range(channels // 8):
        local_ref[8 * i : 8 * i + 8, :] = local[:8, i * channels : (i + 1) * channels]
    bias_ref[...] = local[8:9, :channels] + local[8:9, channels : 2 * channels]


def spectral_kernel(coeffs_ref, grads_ref, out_ref):
    a = pl.program_id(0)
    groups, _, mode_rows, pairs = out_ref.shape
    wide = coeffs_ref.shape[1]
    channels = wide // AG
    coeffs = only(split(coeffs_ref[...]), a, channels)
    grads = spread_o(split(grads_ref[...]), a, channels)
    spread_c = ones_where((2 * wide, pairs), lambda i, j: i % channels == j // channels)
    for q in range(0, pairs, 256):
        product = dot(coeffs, spread_c[:, q : q + 256]) * grads
        out_ref[:, 0, :, q : q + 256] = product.reshape(groups, mode_rows, 256)


GELU_A = math.sqrt(2.0 / math.pi)
GELU_B = GELU_A * 0.044715


def staged(count, stages):
    held = {}
    for tick in range(count + len(stages) - 1):
        for index, stage in enumerate(stages):
            item = tick - index
            if 0 <= item < count:
                held[item] = stage(item, held.get(item))


def layer_kernel(
    got_ref, flat_ref, cotangent_ref, weight_ref, bias_ref, z_ref, y_ref, yt_ref, rep_ref,
    output_ref, hidden_ref, send_ref, held_ref, e2_ref, p1_ref, sums_ref, sems, *, pieces, loops, cells_y,
):
    rows = z_ref.shape[0]
    width = rep_ref.shape[0]
    rows_x = cotangent_ref.shape[1]
    lanes = flat_ref.shape[1] // pieces
    expand_y(got_ref, yt_ref, sums_ref, e2_ref, cells_y)
    mix = spread_weight(rep_ref, weight_ref[...].astype(F32).T.astype(BF16))
    bias = jnp.sum(rep_ref[...].astype(F32) * bias_ref[...], axis=1, keepdims=True)
    bias = jnp.broadcast_to(bias, (width, CHUNK))
    chunks = flat_ref.shape[1] // CHUNK // loops
    per = pieces // loops

    def send_piece(i):
        span = pl.ds(pl.multiple_of(i * lanes, lanes), lanes)
        return pltpu.make_async_copy(held_ref.at[:, :, span], output_ref.at[:, :, span], sems.at[0, i])

    def piece(i, total):
        base = pl.multiple_of(i * (chunks * YC * PITCH), 8)
        z = z_ref[...]
        totals = [total]

        def lanes_of(j):
            return pl.ds(pl.multiple_of((i * chunks + j) * CHUNK, CHUNK), CHUNK)

        def turn(j, _):
            return take_chunk(e2_ref, base, j).T

        def evaluate(j, e2):
            left = jnp.concatenate([e2, mix], 1)
            return dot(left, jnp.concatenate([z, flat_ref[:, lanes_of(j)]], 0)) + bias

        def activate(j, pre):
            own = lanes_of(j)
            square = pre * pre
            half = 0.5 * jnp.tanh(pre * (GELU_A + GELU_B * square)) + 0.5
            held_ref[:, :, own] = (pre * half).astype(BF16).reshape(-1, rows_x, CHUNK)
            slope = half + (half - half * half) * (pre * (2 * GELU_A + 6 * GELU_B * square))
            cot = cotangent_ref[:, :, own].reshape(-1, CHUNK).astype(F32)
            hidden = (cot * slope).astype(BF16)
            hidden_ref[:, own] = hidden
            if (j + 1) % (chunks // per) == 0:
                send_piece(i * per + j // (chunks // per)).start()
            return hidden

        def reduce(j, hidden):
            cells = flat_ref[:, lanes_of(j)]
            sums = dot(jnp.concatenate([z, cells], 0), hidden, NT)
            put_chunk(p1_ref, base, j, sums[:rows])
            totals[0] = totals[0] + sums[rows:]

        staged(chunks, [turn, evaluate, activate, reduce])
        return totals[0]

    total = [lax.fori_loop(0, loops, piece, jnp.zeros((width, width), F32))]
    contract_y(p1_ref, y_ref, sums_ref, cells_y)
    full = total[0]
    flat_row = jnp.sum(p1_ref[pl.ds(0, cells_y, stride=PITCH), :], axis=0, keepdims=True)
    flat_row = jnp.broadcast_to(flat_row / z_ref[0:1, 0:1].astype(F32), (8, width))
    row = lax.broadcasted_iota(jnp.int32, full.shape, 0)
    col = lax.broadcasted_iota(jnp.int32, full.shape, 1)
    full = jnp.where(row % rows_x == col % rows_x, full, 0.0)
    rep = rep_ref[...].astype(F32)
    high = lax.Precision.HIGHEST
    tall = dot(jnp.concatenate([full, flat_row], 0), rep, precision=high)
    channels = rep.shape[1]
    local = dot(rep.T, tall[:width], precision=high)
    tops = [local[i : i + 8] for i in range(0, channels, 8)]
    bias_sum = jnp.broadcast_to(tall[width : width + 1], (8, channels))
    high = bias_sum.astype(BF16).astype(F32)
    blank = jnp.zeros((8, 128 - 2 * channels), F32)
    packed = jnp.concatenate(
        [jnp.concatenate(tops, 1), jnp.concatenate([high, bias_sum - high, blank], 1)], 0
    ).astype(BF16)
    devices = send_ref.shape[0]
    mode_rows = K * K // devices
    for d in range(devices):
        send_ref[d, :mode_rows] = block_of(sums_ref, d, mode_rows)
        send_ref[d, mode_rows:] = packed
    for i in range(pieces):
        send_piece(i).wait()


def field_grad_kernel(
    got_ref, hidden_any, weight_ref, z_ref, yt_ref, rep_ref, output_ref, hidden_ref, held_ref, e2_ref, sums_ref, sems,
    *, cells_y,
):
    rows_x = held_ref.shape[1]
    cells = hidden_ref.shape[1]
    takes = {}
    for k, (first, end) in enumerate(spans_of(PIECES, cells)):
        takes[first // CHUNK] = pltpu.make_async_copy(
            hidden_any.at[:, first:end], hidden_ref.at[:, first:end], sems.at[1, k]
        )
    sends = {}
    for k, (first, end) in enumerate(spans_of(PIECES, cells)):
        sends[end // CHUNK - 1] = pltpu.make_async_copy(
            held_ref.at[:, :, first:end], output_ref.at[:, :, first:end], sems.at[0, k]
        )
    for take in takes.values():
        take.start()
    expand_y(got_ref, yt_ref, sums_ref, e2_ref, cells_y)
    mix = spread_weight(rep_ref, weight_ref[...])
    z = z_ref[...]

    def turn(j, _):
        return take_chunk(e2_ref, 0, j).T

    def evaluate(j, e2):
        left = jnp.concatenate([e2, mix], 1)
        own = slice(j * CHUNK, (j + 1) * CHUNK)
        if j in takes:
            takes[j].wait()
        grad = dot(left, jnp.concatenate([z, hidden_ref[:, own]], 0))
        held_ref[:, :, own] = grad.astype(BF16).reshape(-1, rows_x, CHUNK)
        if j in sends:
            sends[j].start()

    staged(cells // CHUNK, [turn, evaluate])
    for send in sends.values():
        send.wait()


def body(state_field, cotangent, spectral_weight, local_weight, local_bias):
    channels, rows_x, cells = state_field.shape
    cells_y = cells // NZ
    devices = lax.axis_size("gx")
    mode_rows = spectral_weight.shape[1]
    wide = channels * rows_x
    groups = K // AG
    table = tables(channels, rows_x, devices, cells_y)
    in_vmem = pl.BlockSpec(memory_space=pltpu.VMEM)

    def params(mib):
        return pltpu.CompilerParams(vmem_limit_bytes=mib * 1024 * 1024)

    in_any = pl.BlockSpec(memory_space=pl.ANY)
    held = pltpu.VMEM((channels, rows_x, cells), BF16)
    sems = pltpu.SemaphoreType.DMA((2, PIECES))
    field = jax.ShapeDtypeStruct(state_field.shape, BF16)
    flat_field = jax.ShapeDtypeStruct((wide, cells), BF16)

    def cost(moved):
        return pl.CostEstimate(flops=0, bytes_accessed=moved, transcendentals=0)

    blocks = jax.ShapeDtypeStruct((devices, mode_rows, wide), BF16)
    packed = jax.ShapeDtypeStruct((devices, mode_rows + PACK, wide), BF16)
    coeffs_shape = jax.ShapeDtypeStruct((groups * mode_rows, AG * channels), F32)
    p1 = pltpu.VMEM((cells_y * PITCH, wide), F32)
    sums = pltpu.VMEM((K * PITCH, wide), F32)
    weight = spectral_weight.reshape(groups, AG, mode_rows, channels * channels)

    def exchange(values_in):
        return lax.all_to_all(values_in, "gx", 0, 0, tiled=True)

    def in_hbm(array):
        return pltpu.with_memory_space_constraint(array, pltpu.HBM)

    projected, flat, x_table = pl.pallas_call(
        functools.partial(project_kernel, cells_y=cells_y),
        in_specs=[in_any] * 4,
        out_specs=[in_vmem] * 3,
        out_shape=[blocks, flat_field, jax.ShapeDtypeStruct(table["x"].shape, BF16)],
        scratch_shapes=[
            pltpu.VMEM(table["z"].shape, BF16), pltpu.VMEM(table["y"].shape, BF16),
            pltpu.VMEM(table["x_rows"].shape, BF16),
            held, p1, sums, pltpu.SemaphoreType.DMA((5,)),
        ],
        compiler_params=params(18),
        cost_estimate=cost(48 << 20),
        name="project",
    )(in_hbm(state_field), in_hbm(table["z"]), in_hbm(table["y"]), in_hbm(table["x_rows"]))
    got = exchange(projected)
    mixed, coeffs = pl.pallas_call(
        mix_kernel,
        in_specs=[in_vmem] * 3,
        out_specs=[in_vmem] * 2,
        out_shape=[blocks, coeffs_shape],
        compiler_params=params(10),
        cost_estimate=cost(48 << 20),
        name="mix",
    )(got, weight, x_table)
    got = exchange(mixed)
    bias_row = local_bias.reshape(1, channels)
    layer_output, hidden, projected = pl.pallas_call(
        functools.partial(layer_kernel, pieces=PIECES, loops=2, cells_y=cells_y),
        in_specs=[in_vmem] * 9,
        out_specs=[in_any, in_vmem, in_vmem],
        out_shape=[field, flat_field, packed],
        scratch_shapes=[held, p1, p1, sums, sems],
        compiler_params=params(22),
        cost_estimate=cost(64 << 20),
        name="layer",
    )(
        got, flat, cotangent, local_weight, bias_row,
        table["z"], table["y"], table["yt"], table["rep"],
    )
    got = exchange(projected)
    back, grads, local, bias_grad = pl.pallas_call(
        back_kernel,
        in_specs=[in_vmem] * 3,
        out_specs=[in_vmem] * 4,
        out_shape=[
            blocks, coeffs_shape,
            jax.ShapeDtypeStruct((channels, channels), F32), jax.ShapeDtypeStruct((1, channels), F32),
        ],
        compiler_params=params(10),
        cost_estimate=cost(48 << 20),
        name="back",
    )(got, weight, table["x"])
    got = exchange(back)
    pairs = channels * channels
    spectral_grad = pl.pallas_call(
        spectral_kernel,
        grid=(AG,),
        in_specs=[in_vmem, in_vmem],
        out_specs=pl.BlockSpec((groups, 1, mode_rows, pairs), lambda i: (0, i, 0, 0)),
        out_shape=jax.ShapeDtypeStruct((groups, AG, mode_rows, pairs), F32),
        compiler_params=params(10),
        cost_estimate=pl.CostEstimate(
            flops=2 * 256 * K * mode_rows * pairs, bytes_accessed=4 * K * mode_rows * pairs, transcendentals=0
        ),
        name="spectral",
    )(coeffs, grads)
    field_grad = pl.pallas_call(
        functools.partial(field_grad_kernel, cells_y=cells_y),
        in_specs=[in_vmem, in_any] + [in_vmem] * 4,
        out_specs=in_any,
        out_shape=field,
        scratch_shapes=[pltpu.VMEM((wide, cells), BF16), held, p1, sums, sems],
        compiler_params=params(16),
        cost_estimate=cost(48 << 20),
        name="field_grad",
    )(got, in_hbm(hidden), local_weight, table["z"], table["yt"], table["rep"])
    spectral_grad = spectral_grad.reshape(K, mode_rows, pairs)
    return (layer_output, field_grad, spectral_grad, local, bias_grad.reshape(channels))


def solution(mesh):
    placed = (P(None, "gx", "grp"), P(None, "gx", "grp"), P(None, "gx", None), P(), P())
    return jax.shard_map(
        body,
        mesh=mesh,
        in_specs=placed,
        out_specs=(
            P(None, "gx", "grp"),
            P(None, "gx", "grp"),
            P("grp", "gx", None),
            P("grp", None),
            P("grp"),
        ),
        check_vma=False,
    )
```

```python
import functools
import math

import jax
import jax.numpy as jnp
import numpy as np
from jax import lax
from jax.experimental import pallas as pl
from jax.experimental.pallas import tpu as pltpu
from jax.sharding import PartitionSpec as P

MODES = 16
K = 2 * MODES
NZ = 64
YC = 4
CHUNK = YC * NZ
AG = 4
SUB = 8
PIECES = 4
PITCH = K + 1
PACK = 16
F32 = jnp.float32
BF16 = jnp.bfloat16
NN = (((1,), (0,)), ((), ()))
NT = (((1,), (1,)), ((), ()))


def dot(lhs, rhs, dims=NN, precision=None):
    return lax.dot_general(lhs, rhs, dims, precision=precision, preferred_element_type=F32)


def basis_table(length):
    cells = np.arange(length)
    rows = np.arange(K)
    frequency = np.where(rows < MODES, rows, rows - MODES + 1)
    phase_index = frequency[:, None] * cells[None, :] % length
    angles = phase_index.astype(np.float32) * np.float32(2.0 * math.pi / length)
    angles = angles.astype(np.float64)
    table = np.where((rows < MODES)[:, None], np.cos(angles), np.sin(angles))
    return (table * math.sqrt(2.0 / length)).astype(np.float32)


def halves(table):
    high = table.astype(BF16)
    low = (table - high.astype(np.float32)).astype(BF16)
    return high, low


def tables(channels, rows_x, devices, cells_y):
    table_x = basis_table(rows_x * devices)
    y_high, y_low = halves(basis_table(cells_y))
    z = basis_table(NZ).astype(BF16).astype(np.float32)
    eye_c = np.eye(channels, dtype=np.float32)
    out = {}
    out["z"] = np.kron(np.eye(YC, dtype=np.float32), z).astype(BF16)
    out["y"] = np.concatenate([y_high, y_low], 0)
    out["yt"] = np.concatenate([y_high.T, y_low.T], 1)
    out["rep"] = np.kron(eye_c, np.ones((rows_x, 1), np.float32)).astype(BF16)
    x = np.stack(halves(table_x)).astype(np.float32).reshape(2, K, devices, rows_x)
    x = np.einsum("hadx,ce->dexhac", x, np.eye(SUB, dtype=np.float32))
    out["x"] = x.reshape(devices * SUB * rows_x, 2 * K * SUB).astype(BF16)
    return {name: jnp.asarray(value) for name, value in out.items()}


def split(values_in):
    high = values_in.astype(BF16)
    low = (values_in - high.astype(F32)).astype(BF16)
    return jnp.concatenate([high, low], 1)


def put_chunk(ref, base, index, values_in):
    for i in range(YC):
        ref[pl.ds(base + (index * YC + i) * PITCH, K), :] = values_in[i * K : (i + 1) * K]


def take_chunk(ref, base, index):
    parts = [ref[pl.ds(base + (index * YC + i) * PITCH, K), :] for i in range(YC)]
    return jnp.concatenate(parts, 0).astype(BF16)


def contract_y(p1_ref, y_ref, sums_ref, cells_y):
    y = y_ref[...]
    width = p1_ref.shape[1]
    for g in range(0, K, 2):
        pair = [p1_ref[pl.ds(g + i, cells_y, stride=PITCH), :].astype(BF16) for i in range(2)]
        both = dot(y, jnp.concatenate(pair, 1))
        both = both[:K] + both[K:]
        for i in range(2):
            sums_ref[pl.ds(g + i, K, stride=PITCH), :] = both[:, i * width : (i + 1) * width]


def block_of(sums_ref, index, mode_rows):
    first = index * (mode_rows // K)
    parts = [sums_ref[(first + i) * PITCH : (first + i) * PITCH + K, :] for i in range(mode_rows // K)]
    return jnp.concatenate(parts, 0).astype(BF16)


def expand_y(got_ref, yt_ref, sums_ref, e2_ref, cells_y):
    devices, mode_rows, width = got_ref.shape
    for d in range(devices):
        block = got_ref[d].astype(F32)
        for i in range(mode_rows // K):
            first = (d * (mode_rows // K) + i) * PITCH
            sums_ref[first : first + K, :] = block[i * K : (i + 1) * K]
    yt = yt_ref[...]
    for g in range(0, K, 2):
        pair = [sums_ref[pl.ds(g + i, K, stride=PITCH), :].astype(BF16) for i in range(2)]
        rhs = jnp.concatenate(pair, 1)
        both = dot(yt, jnp.concatenate([rhs, rhs], 0))
        for i in range(2):
            e2_ref[pl.ds(g + i, cells_y, stride=PITCH), :] = both[:, i * width : (i + 1) * width]


def spread_weight(rep_ref, weight):
    rep = rep_ref[...]
    wide = dot(dot(rep, weight).astype(BF16), rep, NT)
    rows_x = rep.shape[0] // rep.shape[1]
    row = lax.broadcasted_iota(jnp.int32, wide.shape, 0)
    col = lax.broadcasted_iota(jnp.int32, wide.shape, 1)
    return jnp.where(row % rows_x == col % rows_x, wide, 0.0).astype(BF16)


def spans_of(pieces, cells):
    return [(i * (cells // pieces), (i + 1) * (cells // pieces)) for i in range(pieces)]


def project_kernel(
    state_ref, z_any, y_any, x_any, out_ref, flat_ref, x_ref, z_ref, y_ref, held_ref, p1_ref, sums_ref, sems, *, cells_y
):
    cells = state_ref.shape[2]
    pieces = [
        pltpu.make_async_copy(state_ref.at[:, :, first:end], held_ref.at[:, :, first:end], sems.at[k])
        for k, (first, end) in enumerate(spans_of(2, cells))
    ]
    starts = {first // CHUNK: piece for (first, _), piece in zip(spans_of(2, cells), pieces, strict=True)}
    copy_z = pltpu.make_async_copy(z_any, z_ref, sems.at[2])
    copy_y = pltpu.make_async_copy(y_any, y_ref, sems.at[3])
    copy_z.start()
    for piece in pieces:
        piece.start()
    copy_x = pltpu.make_async_copy(x_any, x_ref, sems.at[4])
    copy_y.start()
    copy_x.start()
    copy_z.wait()
    z = z_ref[...]
    for j in range(cells // CHUNK):
        if j in starts:
            starts[j].wait()
        own = slice(j * CHUNK, (j + 1) * CHUNK)
        block = held_ref[:, :, own].reshape(-1, CHUNK)
        flat_ref[:, own] = block
        put_chunk(p1_ref, 0, j, dot(z, block, NT))
    copy_y.wait()
    contract_y(p1_ref, y_ref, sums_ref, cells_y)
    devices, mode_rows, _ = out_ref.shape
    for d in range(devices):
        out_ref[d] = block_of(sums_ref, d, mode_rows)
    copy_x.wait()


def regroup(tiles):
    lane = lax.broadcasted_iota(jnp.int32, tiles[0].shape, 1)
    quarter = 128 // len(tiles)
    result = []
    for q in range(len(tiles)):
        whole = tiles[q]
        for i in range(len(tiles)):
            if i != q:
                moved = pltpu.roll(tiles[i], (i - q) * quarter % 128, 1)
                whole = jnp.where(lane // quarter == i, moved, whole)
        result.append(whole)
    return result


def sum_x(got_ref, x_ref, coeffs_ref, mode_rows):
    devices = got_ref.shape[0]
    quads = [
        regroup([got_ref[d + i, :mode_rows].astype(F32) for i in range(4)]) for d in range(0, devices, 4)
    ]
    left = [jnp.concatenate([quad[c].astype(BF16) for quad in quads], 1) for c in range(4)]
    both = dot(jnp.concatenate(left, 0), x_ref[...])
    coeffs = both[:, : K * SUB] + both[:, K * SUB :]
    for h in range(0, K * SUB, 128):
        tiles = regroup([coeffs[c * mode_rows : (c + 1) * mode_rows, h : h + 128] for c in range(4)])
        for q, tile in enumerate(tiles):
            t = h // 128 * 4 + q
            coeffs_ref[t * mode_rows : (t + 1) * mode_rows, :] = tile


def spread_x(modes, x_ref, send_ref):
    devices, mode_rows, _ = send_ref.shape
    modes = modes.astype(F32)
    quads = [
        regroup([modes[t * mode_rows : (t + 1) * mode_rows] for t in range(h, h + 4)]) for h in range(0, K // AG, 4)
    ]
    left = jnp.concatenate([jnp.concatenate([quad[c].astype(BF16) for quad in quads], 1) for c in range(4)], 0)
    values = dot(jnp.concatenate([left, left], 1), x_ref[...], NT)
    for d in range(0, devices, 4):
        lanes = slice(d * 32, d * 32 + 128)
        tiles = regroup([values[c * mode_rows : (c + 1) * mode_rows, lanes] for c in range(4)])
        for i, tile in enumerate(tiles):
            send_ref[d + i] = tile.astype(BF16)


def lane_a(lane):
    return lane // SUB % AG


def lane_c(lane):
    return lane // (SUB * AG) % 4 * SUB + lane % SUB


def ones_where(shape, test):
    row = lax.broadcasted_iota(jnp.int32, shape, 0)
    col = lax.broadcasted_iota(jnp.int32, shape, 1)
    return jnp.where(test(row, col), 1.0, 0.0).astype(BF16)


def only(values_in, a):
    lane = lax.broadcasted_iota(jnp.int32, values_in.shape, 1)
    return jnp.where(lane_a(lane) == a, values_in, jnp.zeros_like(values_in))


def mix_kernel(got_ref, weight_ref, x_ref, send_ref, coeffs_ref):
    mode_rows, pairs = weight_ref.shape[2:]
    rows, wide = coeffs_ref.shape
    channels = wide // AG
    sum_x(got_ref, x_ref, coeffs_ref, mode_rows)
    left = split(coeffs_ref[...])
    spread_c = ones_where((2 * wide, pairs), lambda i, j: lane_c(i) == j // channels)
    parts = []
    for a in range(AG):
        own = only(left, a)
        total = None
        for q in range(0, pairs, 256):
            weight = weight_ref[:, a, :, q : q + 256].reshape(rows, 256).astype(F32)
            product = dot(own, spread_c[:, q : q + 256]) * weight
            product = product[:, :128] + product[:, 128:]
            total = product if total is None else total + product
        parts.append(split(total))
    fold = ones_where((AG * 256, wide), lambda i, j: (i // 256 == lane_a(j)) & (i % channels == lane_c(j)))
    mixed = dot(jnp.concatenate(parts, 1), fold).astype(BF16)
    spread_x(mixed, x_ref, send_ref)


def spread_o(grads, a, channels):
    pick = ones_where((grads.shape[1], 128), lambda i, j: lane_c(i) == j % channels)
    wide = dot(only(grads, a), pick)
    return jnp.concatenate([wide, wide], 1)


def back_kernel(got_ref, weight_ref, x_ref, send_ref, grads_ref, local_ref, bias_ref):
    mode_rows, pairs = weight_ref.shape[2:]
    rows, wide = grads_ref.shape
    channels = wide // AG
    sum_x(got_ref, x_ref, grads_ref, mode_rows)
    left = split(grads_ref[...])
    fold = ones_where((pairs, wide), lambda i, j: i // channels == lane_c(j))
    back = None
    for a in range(AG):
        grads = spread_o(left, a, channels)
        products = []
        for q in range(0, pairs, 256):
            weight = weight_ref[:, a, :, q : q + 256].reshape(rows, 256).astype(F32)
            products.append((grads * weight).astype(BF16))
        part = only(dot(jnp.concatenate(products, 1), fold), a)
        back = part if back is None else back + part
    spread_x(back.astype(BF16), x_ref, send_ref)
    local = got_ref[0, mode_rows:].astype(F32)
    for d in range(1, got_ref.shape[0]):
        local = local + got_ref[d, mode_rows:].astype(F32)
    for i in range(channels // 8):
        local_ref[8 * i : 8 * i + 8, :] = local[:8, i * channels : (i + 1) * channels]
    bias_ref[...] = local[8:9, :channels] + local[8:9, channels : 2 * channels]


def spectral_kernel(coeffs_ref, grads_ref, out_ref):
    a = pl.program_id(0)
    groups, _, mode_rows, pairs = out_ref.shape
    wide = coeffs_ref.shape[1]
    channels = wide // AG
    coeffs = only(split(coeffs_ref[...]), a)
    grads = spread_o(split(grads_ref[...]), a, channels)
    spread_c = ones_where((2 * wide, pairs), lambda i, j: lane_c(i) == j // channels)
    for q in range(0, pairs, 256):
        product = dot(coeffs, spread_c[:, q : q + 256]) * grads
        out_ref[:, 0, :, q : q + 256] = product.reshape(groups, mode_rows, 256)


GELU_A = math.sqrt(2.0 / math.pi)
GELU_B = GELU_A * 0.044715


def staged(count, stages):
    held = {}
    for tick in range(count + len(stages) - 1):
        for index, stage in enumerate(stages):
            item = tick - index
            if 0 <= item < count:
                held[item] = stage(item, held.get(item))


def layer_kernel(
    got_ref, flat_ref, cotangent_ref, weight_ref, bias_ref, z_ref, y_ref, yt_ref, rep_ref,
    output_ref, hidden_ref, send_ref, held_ref, e2_ref, p1_ref, sums_ref, sems, *, pieces, loops, cells_y,
):
    rows = z_ref.shape[0]
    width = rep_ref.shape[0]
    rows_x = cotangent_ref.shape[1]
    lanes = flat_ref.shape[1] // pieces
    expand_y(got_ref, yt_ref, sums_ref, e2_ref, cells_y)
    mix = spread_weight(rep_ref, weight_ref[...].astype(F32).T.astype(BF16))
    bias = jnp.sum(rep_ref[...].astype(F32) * bias_ref[...], axis=1, keepdims=True)
    bias = jnp.broadcast_to(bias, (width, CHUNK))
    chunks = flat_ref.shape[1] // CHUNK // loops
    per = pieces // loops

    def send_piece(i):
        span = pl.ds(pl.multiple_of(i * lanes, lanes), lanes)
        return pltpu.make_async_copy(held_ref.at[:, :, span], output_ref.at[:, :, span], sems.at[0, i])

    def piece(i, total):
        base = pl.multiple_of(i * (chunks * YC * PITCH), 8)
        z = z_ref[...]
        totals = [total]

        def lanes_of(j):
            return pl.ds(pl.multiple_of((i * chunks + j) * CHUNK, CHUNK), CHUNK)

        def turn(j, _):
            return take_chunk(e2_ref, base, j).T

        def evaluate(j, e2):
            left = jnp.concatenate([e2, mix], 1)
            return dot(left, jnp.concatenate([z, flat_ref[:, lanes_of(j)]], 0)) + bias

        def activate(j, pre):
            own = lanes_of(j)
            square = pre * pre
            half = 0.5 * jnp.tanh(pre * (GELU_A + GELU_B * square)) + 0.5
            held_ref[:, :, own] = (pre * half).astype(BF16).reshape(-1, rows_x, CHUNK)
            slope = half + (half - half * half) * (pre * (2 * GELU_A + 6 * GELU_B * square))
            cot = cotangent_ref[:, :, own].reshape(-1, CHUNK).astype(F32)
            hidden = (cot * slope).astype(BF16)
            hidden_ref[:, own] = hidden
            if (j + 1) % (chunks // per) == 0:
                send_piece(i * per + j // (chunks // per)).start()
            return hidden

        def reduce(j, hidden):
            cells = flat_ref[:, lanes_of(j)]
            sums = dot(jnp.concatenate([z, cells], 0), hidden, NT)
            put_chunk(p1_ref, base, j, sums[:rows])
            totals[0] = totals[0] + sums[rows:]

        staged(chunks, [turn, evaluate, activate, reduce])
        return totals[0]

    total = [lax.fori_loop(0, loops, piece, jnp.zeros((width, width), F32))]
    contract_y(p1_ref, y_ref, sums_ref, cells_y)
    full = total[0]
    flat_row = jnp.sum(p1_ref[pl.ds(0, cells_y, stride=PITCH), :], axis=0, keepdims=True)
    flat_row = jnp.broadcast_to(flat_row / z_ref[0:1, 0:1].astype(F32), (8, width))
    row = lax.broadcasted_iota(jnp.int32, full.shape, 0)
    col = lax.broadcasted_iota(jnp.int32, full.shape, 1)
    full = jnp.where(row % rows_x == col % rows_x, full, 0.0)
    rep = rep_ref[...].astype(F32)
    high = lax.Precision.HIGHEST
    tall = dot(jnp.concatenate([full, flat_row], 0), rep, precision=high)
    channels = rep.shape[1]
    local = dot(rep.T, tall[:width], precision=high)
    tops = [local[i : i + 8] for i in range(0, channels, 8)]
    bias_sum = jnp.broadcast_to(tall[width : width + 1], (8, channels))
    high = bias_sum.astype(BF16).astype(F32)
    blank = jnp.zeros((8, 128 - 2 * channels), F32)
    packed = jnp.concatenate(
        [jnp.concatenate(tops, 1), jnp.concatenate([high, bias_sum - high, blank], 1)], 0
    ).astype(BF16)
    devices = send_ref.shape[0]
    mode_rows = K * K // devices
    for d in range(devices):
        send_ref[d, :mode_rows] = block_of(sums_ref, d, mode_rows)
        send_ref[d, mode_rows:] = packed
    for i in range(pieces):
        send_piece(i).wait()


def field_grad_kernel(
    got_ref, hidden_any, weight_ref, z_ref, yt_ref, rep_ref, output_ref, hidden_ref, held_ref, e2_ref, sums_ref, sems,
    *, cells_y,
):
    rows_x = held_ref.shape[1]
    cells = hidden_ref.shape[1]
    takes = {}
    for k, (first, end) in enumerate(spans_of(PIECES, cells)):
        takes[first // CHUNK] = pltpu.make_async_copy(
            hidden_any.at[:, first:end], hidden_ref.at[:, first:end], sems.at[1, k]
        )
    sends = {}
    for k, (first, end) in enumerate(spans_of(PIECES, cells)):
        sends[end // CHUNK - 1] = pltpu.make_async_copy(
            held_ref.at[:, :, first:end], output_ref.at[:, :, first:end], sems.at[0, k]
        )
    for take in takes.values():
        take.start()
    expand_y(got_ref, yt_ref, sums_ref, e2_ref, cells_y)
    mix = spread_weight(rep_ref, weight_ref[...])
    z = z_ref[...]

    def turn(j, _):
        return take_chunk(e2_ref, 0, j).T

    def evaluate(j, e2):
        left = jnp.concatenate([e2, mix], 1)
        own = slice(j * CHUNK, (j + 1) * CHUNK)
        if j in takes:
            takes[j].wait()
        grad = dot(left, jnp.concatenate([z, hidden_ref[:, own]], 0))
        held_ref[:, :, own] = grad.astype(BF16).reshape(-1, rows_x, CHUNK)
        if j in sends:
            sends[j].start()

    staged(cells // CHUNK, [turn, evaluate])
    for send in sends.values():
        send.wait()


def body(state_field, cotangent, spectral_weight, local_weight, local_bias):
    channels, rows_x, cells = state_field.shape
    cells_y = cells // NZ
    devices = lax.axis_size("gx")
    mode_rows = spectral_weight.shape[1]
    wide = channels * rows_x
    groups = K // AG
    table = tables(channels, rows_x, devices, cells_y)
    in_vmem = pl.BlockSpec(memory_space=pltpu.VMEM)

    def params(mib):
        return pltpu.CompilerParams(vmem_limit_bytes=mib * 1024 * 1024)

    in_any = pl.BlockSpec(memory_space=pl.ANY)
    held = pltpu.VMEM((channels, rows_x, cells), BF16)
    sems = pltpu.SemaphoreType.DMA((2, PIECES))
    field = jax.ShapeDtypeStruct(state_field.shape, BF16)
    flat_field = jax.ShapeDtypeStruct((wide, cells), BF16)

    def cost(moved):
        return pl.CostEstimate(flops=0, bytes_accessed=moved, transcendentals=0)

    blocks = jax.ShapeDtypeStruct((devices, mode_rows, wide), BF16)
    packed = jax.ShapeDtypeStruct((devices, mode_rows + PACK, wide), BF16)
    coeffs_shape = jax.ShapeDtypeStruct((groups * mode_rows, AG * channels), F32)
    p1 = pltpu.VMEM((cells_y * PITCH, wide), F32)
    sums = pltpu.VMEM((K * PITCH, wide), F32)
    weight = spectral_weight.reshape(groups, AG, mode_rows, channels * channels)

    def exchange(values_in):
        return lax.all_to_all(values_in, "gx", 0, 0, tiled=True)

    def in_hbm(array):
        return pltpu.with_memory_space_constraint(array, pltpu.HBM)

    projected, flat, x_table = pl.pallas_call(
        functools.partial(project_kernel, cells_y=cells_y),
        in_specs=[in_any] * 4,
        out_specs=[in_vmem] * 3,
        out_shape=[blocks, flat_field, jax.ShapeDtypeStruct(table["x"].shape, BF16)],
        scratch_shapes=[
            pltpu.VMEM(table["z"].shape, BF16), pltpu.VMEM(table["y"].shape, BF16),
            held, p1, sums, pltpu.SemaphoreType.DMA((5,)),
        ],
        compiler_params=params(18),
        cost_estimate=cost(48 << 20),
        name="project",
    )(in_hbm(state_field), in_hbm(table["z"]), in_hbm(table["y"]), in_hbm(table["x"]))
    got = exchange(projected)
    mixed, coeffs = pl.pallas_call(
        mix_kernel,
        in_specs=[in_vmem] * 3,
        out_specs=[in_vmem] * 2,
        out_shape=[blocks, coeffs_shape],
        compiler_params=params(10),
        cost_estimate=cost(48 << 20),
        name="mix",
    )(got, weight, x_table)
    got = exchange(mixed)
    bias_row = local_bias.reshape(1, channels)
    layer_output, hidden, projected = pl.pallas_call(
        functools.partial(layer_kernel, pieces=PIECES, loops=2, cells_y=cells_y),
        in_specs=[in_vmem] * 9,
        out_specs=[in_any, in_vmem, in_vmem],
        out_shape=[field, flat_field, packed],
        scratch_shapes=[held, p1, p1, sums, sems],
        compiler_params=params(22),
        cost_estimate=cost(64 << 20),
        name="layer",
    )(
        got, flat, cotangent, local_weight, bias_row,
        table["z"], table["y"], table["yt"], table["rep"],
    )
    got = exchange(projected)
    back, grads, local, bias_grad = pl.pallas_call(
        back_kernel,
        in_specs=[in_vmem] * 3,
        out_specs=[in_vmem] * 4,
        out_shape=[
            blocks, coeffs_shape,
            jax.ShapeDtypeStruct((channels, channels), F32), jax.ShapeDtypeStruct((1, channels), F32),
        ],
        compiler_params=params(10),
        cost_estimate=cost(48 << 20),
        name="back",
    )(got, weight, x_table)
    got = exchange(back)
    pairs = channels * channels
    spectral_grad = pl.pallas_call(
        spectral_kernel,
        grid=(AG,),
        in_specs=[in_vmem, in_vmem],
        out_specs=pl.BlockSpec((groups, 1, mode_rows, pairs), lambda i: (0, i, 0, 0)),
        out_shape=jax.ShapeDtypeStruct((groups, AG, mode_rows, pairs), F32),
        compiler_params=params(10),
        cost_estimate=pl.CostEstimate(
            flops=2 * 256 * K * mode_rows * pairs, bytes_accessed=4 * K * mode_rows * pairs, transcendentals=0
        ),
        name="spectral",
    )(coeffs, grads)
    field_grad = pl.pallas_call(
        functools.partial(field_grad_kernel, cells_y=cells_y),
        in_specs=[in_vmem, in_any] + [in_vmem] * 4,
        out_specs=in_any,
        out_shape=field,
        scratch_shapes=[pltpu.VMEM((wide, cells), BF16), held, p1, sums, sems],
        compiler_params=params(16),
        cost_estimate=cost(48 << 20),
        name="field_grad",
    )(got, in_hbm(hidden), local_weight, table["z"], table["yt"], table["rep"])
    spectral_grad = spectral_grad.reshape(K, mode_rows, pairs)
    return (layer_output, field_grad, spectral_grad, local, bias_grad.reshape(channels))


def solution(mesh):
    placed = (P(None, "gx", "grp"), P(None, "gx", "grp"), P(None, "gx", None), P(), P())
    return jax.shard_map(
        body,
        mesh=mesh,
        in_specs=placed,
        out_specs=(
            P(None, "gx", "grp"),
            P(None, "gx", "grp"),
            P("grp", "gx", None),
            P("grp", None),
            P("grp"),
        ),
        check_vma=False,
    )
```

```python
import functools
import math

import jax
import jax.numpy as jnp
import numpy as np
from jax import lax
from jax.experimental import pallas as pl
from jax.experimental.pallas import tpu as pltpu
from jax.sharding import PartitionSpec as P

MODES = 16
K = 2 * MODES
NZ = 64
YC = 4
CHUNK = YC * NZ
AG = 4
SUB = 8
PIECES = 4
PITCH = K + 1
PACK = 16
F32 = jnp.float32
BF16 = jnp.bfloat16
NN = (((1,), (0,)), ((), ()))
NT = (((1,), (1,)), ((), ()))


def dot(lhs, rhs, dims=NN, precision=None):
    return lax.dot_general(lhs, rhs, dims, precision=precision, preferred_element_type=F32)


def basis_table(length):
    cells = np.arange(length)
    rows = np.arange(K)
    frequency = np.where(rows < MODES, rows, rows - MODES + 1)
    phase_index = frequency[:, None] * cells[None, :] % length
    angles = phase_index.astype(np.float32) * np.float32(2.0 * math.pi / length)
    angles = angles.astype(np.float64)
    table = np.where((rows < MODES)[:, None], np.cos(angles), np.sin(angles))
    return (table * math.sqrt(2.0 / length)).astype(np.float32)


def halves(table):
    high = table.astype(BF16)
    low = (table - high.astype(np.float32)).astype(BF16)
    return high, low


def tables(channels, rows_x, devices, cells_y):
    table_x = basis_table(rows_x * devices)
    y_high, y_low = halves(basis_table(cells_y))
    z = basis_table(NZ).astype(BF16).astype(np.float32)
    eye_c = np.eye(channels, dtype=np.float32)
    out = {}
    out["z"] = np.kron(np.eye(YC, dtype=np.float32), z).astype(BF16)
    out["y"] = np.concatenate([y_high, y_low], 0)
    out["yt"] = np.concatenate([y_high.T, y_low.T], 1)
    out["rep"] = np.kron(eye_c, np.ones((rows_x, 1), np.float32)).astype(BF16)
    x = np.stack(halves(table_x)).astype(np.float32).reshape(2, K, devices, rows_x)
    x = np.einsum("hadx,ce->dexhac", x, np.eye(SUB, dtype=np.float32))
    out["x"] = x.reshape(devices * SUB * rows_x, 2 * K * SUB).astype(BF16)
    return {name: jnp.asarray(value) for name, value in out.items()}


def split(values_in):
    high = values_in.astype(BF16)
    low = (values_in - high.astype(F32)).astype(BF16)
    return jnp.concatenate([high, low], 1)


def put_chunk(ref, base, index, values_in):
    for i in range(YC):
        ref[pl.ds(base + (index * YC + i) * PITCH, K), :] = values_in[i * K : (i + 1) * K]


def take_chunk(ref, base, index):
    parts = [ref[pl.ds(base + (index * YC + i) * PITCH, K), :] for i in range(YC)]
    return jnp.concatenate(parts, 0).astype(BF16)


def contract_y(p1_ref, y_ref, sums_ref, cells_y):
    y = y_ref[...]
    width = p1_ref.shape[1]
    for g in range(0, K, 2):
        pair = [p1_ref[pl.ds(g + i, cells_y, stride=PITCH), :].astype(BF16) for i in range(2)]
        both = dot(y, jnp.concatenate(pair, 1))
        both = both[:K] + both[K:]
        for i in range(2):
            sums_ref[pl.ds(g + i, K, stride=PITCH), :] = both[:, i * width : (i + 1) * width]


def block_of(sums_ref, index, mode_rows):
    first = index * (mode_rows // K)
    parts = [sums_ref[(first + i) * PITCH : (first + i) * PITCH + K, :] for i in range(mode_rows // K)]
    return jnp.concatenate(parts, 0).astype(BF16)


def expand_y(got_ref, yt_ref, sums_ref, e2_ref, cells_y):
    devices, mode_rows, width = got_ref.shape
    for d in range(devices):
        block = got_ref[d].astype(F32)
        for i in range(mode_rows // K):
            first = (d * (mode_rows // K) + i) * PITCH
            sums_ref[first : first + K, :] = block[i * K : (i + 1) * K]
    yt = yt_ref[...]
    for g in range(0, K, 2):
        pair = [sums_ref[pl.ds(g + i, K, stride=PITCH), :].astype(BF16) for i in range(2)]
        rhs = jnp.concatenate(pair, 1)
        both = dot(yt, jnp.concatenate([rhs, rhs], 0))
        for i in range(2):
            e2_ref[pl.ds(g + i, cells_y, stride=PITCH), :] = both[:, i * width : (i + 1) * width]


def spread_weight(rep_ref, weight):
    rep = rep_ref[...]
    wide = dot(dot(rep, weight).astype(BF16), rep, NT)
    rows_x = rep.shape[0] // rep.shape[1]
    row = lax.broadcasted_iota(jnp.int32, wide.shape, 0)
    col = lax.broadcasted_iota(jnp.int32, wide.shape, 1)
    return jnp.where(row % rows_x == col % rows_x, wide, 0.0).astype(BF16)


def spans_of(pieces, cells):
    return [(i * (cells // pieces), (i + 1) * (cells // pieces)) for i in range(pieces)]


def project_kernel(
    state_ref, z_any, y_any, x_any, out_ref, flat_ref, x_ref, z_ref, y_ref, held_ref, p1_ref, sums_ref, sems, *, cells_y
):
    cells = state_ref.shape[2]
    pieces = [
        pltpu.make_async_copy(state_ref.at[:, :, first:end], held_ref.at[:, :, first:end], sems.at[k])
        for k, (first, end) in enumerate(spans_of(2, cells))
    ]
    starts = {first // CHUNK: piece for (first, _), piece in zip(spans_of(2, cells), pieces, strict=True)}
    copy_z = pltpu.make_async_copy(z_any, z_ref, sems.at[2])
    copy_y = pltpu.make_async_copy(y_any, y_ref, sems.at[3])
    copy_z.start()
    for piece in pieces:
        piece.start()
    copy_x = pltpu.make_async_copy(x_any, x_ref, sems.at[4])
    copy_y.start()
    copy_x.start()
    copy_z.wait()
    z = z_ref[...]
    for j in range(cells // CHUNK):
        if j in starts:
            starts[j].wait()
        own = slice(j * CHUNK, (j + 1) * CHUNK)
        block = held_ref[:, :, own].reshape(-1, CHUNK)
        flat_ref[:, own] = block
        put_chunk(p1_ref, 0, j, dot(z, block, NT))
    copy_y.wait()
    contract_y(p1_ref, y_ref, sums_ref, cells_y)
    devices, mode_rows, _ = out_ref.shape
    for d in range(devices):
        out_ref[d] = block_of(sums_ref, d, mode_rows)
    copy_x.wait()


def regroup(tiles):
    quarter = 128 // len(tiles)
    lane = lax.broadcasted_iota(jnp.int32, tiles[0].shape, 1)
    for bit in (1, 2):
        swapped = []
        for i, tile in enumerate(tiles):
            up = i & bit == 0
            moved = pltpu.roll(tiles[i ^ bit], (bit if up else 4 - bit) * quarter, 1)
            odd = lane // (quarter * bit) % 2 == 1
            swapped.append(jnp.where(odd, moved, tile) if up else jnp.where(odd, tile, moved))
        tiles = swapped
    return tiles


def sum_x(got_ref, x_ref, coeffs_ref, mode_rows):
    devices = got_ref.shape[0]
    quads = [
        regroup([got_ref[d + i, :mode_rows].astype(F32) for i in range(4)]) for d in range(0, devices, 4)
    ]
    left = [jnp.concatenate([quad[c].astype(BF16) for quad in quads], 1) for c in range(4)]
    both = dot(jnp.concatenate(left, 0), x_ref[...])
    coeffs = both[:, : K * SUB] + both[:, K * SUB :]
    for h in range(0, K * SUB, 128):
        tiles = regroup([coeffs[c * mode_rows : (c + 1) * mode_rows, h : h + 128] for c in range(4)])
        for q, tile in enumerate(tiles):
            t = h // 128 * 4 + q
            coeffs_ref[t * mode_rows : (t + 1) * mode_rows, :] = tile


def spread_x(modes, x_ref, send_ref):
    devices, mode_rows, _ = send_ref.shape
    modes = modes.astype(F32)
    quads = [
        regroup([modes[t * mode_rows : (t + 1) * mode_rows] for t in range(h, h + 4)]) for h in range(0, K // AG, 4)
    ]
    left = jnp.concatenate([jnp.concatenate([quad[c].astype(BF16) for quad in quads], 1) for c in range(4)], 0)
    values = dot(jnp.concatenate([left, left], 1), x_ref[...], NT)
    for d in range(0, devices, 4):
        lanes = slice(d * 32, d * 32 + 128)
        tiles = regroup([values[c * mode_rows : (c + 1) * mode_rows, lanes] for c in range(4)])
        for i, tile in enumerate(tiles):
            send_ref[d + i] = tile.astype(BF16)


def lane_a(lane):
    return lane // SUB % AG


def lane_c(lane):
    return lane // (SUB * AG) % 4 * SUB + lane % SUB


def ones_where(shape, test):
    row = lax.broadcasted_iota(jnp.int32, shape, 0)
    col = lax.broadcasted_iota(jnp.int32, shape, 1)
    return jnp.where(test(row, col), 1.0, 0.0).astype(BF16)


def only(values_in, a):
    lane = lax.broadcasted_iota(jnp.int32, values_in.shape, 1)
    return jnp.where(lane_a(lane) == a, values_in, jnp.zeros_like(values_in))


def mix_kernel(got_ref, weight_ref, x_ref, send_ref, coeffs_ref):
    mode_rows, pairs = weight_ref.shape[2:]
    rows, wide = coeffs_ref.shape
    channels = wide // AG
    sum_x(got_ref, x_ref, coeffs_ref, mode_rows)
    left = split(coeffs_ref[...])
    spread_c = ones_where((2 * wide, pairs), lambda i, j: lane_c(i) == j // channels)
    parts = []
    for a in range(AG):
        own = only(left, a)
        total = None
        for q in range(0, pairs, 256):
            weight = weight_ref[:, a, :, q : q + 256].reshape(rows, 256).astype(F32)
            product = dot(own, spread_c[:, q : q + 256]) * weight
            product = product[:, :128] + product[:, 128:]
            total = product if total is None else total + product
        parts.append(split(total))
    fold = ones_where((AG * 256, wide), lambda i, j: (i // 256 == lane_a(j)) & (i % channels == lane_c(j)))
    mixed = dot(jnp.concatenate(parts, 1), fold).astype(BF16)
    spread_x(mixed, x_ref, send_ref)


def spread_o(grads, a, channels):
    pick = ones_where((grads.shape[1], 128), lambda i, j: lane_c(i) == j % channels)
    wide = dot(only(grads, a), pick)
    return jnp.concatenate([wide, wide], 1)


def back_kernel(got_ref, weight_ref, x_ref, send_ref, grads_ref, local_ref, bias_ref):
    mode_rows, pairs = weight_ref.shape[2:]
    rows, wide = grads_ref.shape
    channels = wide // AG
    sum_x(got_ref, x_ref, grads_ref, mode_rows)
    left = split(grads_ref[...])
    fold = ones_where((pairs, wide), lambda i, j: i // channels == lane_c(j))
    back = None
    for a in range(AG):
        grads = spread_o(left, a, channels)
        products = []
        for q in range(0, pairs, 256):
            weight = weight_ref[:, a, :, q : q + 256].reshape(rows, 256).astype(F32)
            products.append((grads * weight).astype(BF16))
        part = only(dot(jnp.concatenate(products, 1), fold), a)
        back = part if back is None else back + part
    spread_x(back.astype(BF16), x_ref, send_ref)
    local = got_ref[0, mode_rows:].astype(F32)
    for d in range(1, got_ref.shape[0]):
        local = local + got_ref[d, mode_rows:].astype(F32)
    for i in range(channels // 8):
        local_ref[8 * i : 8 * i + 8, :] = local[:8, i * channels : (i + 1) * channels]
    bias_ref[...] = local[8:9, :channels] + local[8:9, channels : 2 * channels]


def spectral_kernel(coeffs_ref, grads_ref, out_ref):
    a = pl.program_id(0)
    groups, _, mode_rows, pairs = out_ref.shape
    wide = coeffs_ref.shape[1]
    channels = wide // AG
    coeffs = only(split(coeffs_ref[...]), a)
    grads = spread_o(split(grads_ref[...]), a, channels)
    spread_c = ones_where((2 * wide, pairs), lambda i, j: lane_c(i) == j // channels)
    for q in range(0, pairs, 256):
        product = dot(coeffs, spread_c[:, q : q + 256]) * grads
        out_ref[:, 0, :, q : q + 256] = product.reshape(groups, mode_rows, 256)


GELU_A = math.sqrt(2.0 / math.pi)
GELU_B = GELU_A * 0.044715


def staged(count, stages):
    held = {}
    for tick in range(count + len(stages) - 1):
        for index, stage in enumerate(stages):
            item = tick - index
            if 0 <= item < count:
                held[item] = stage(item, held.get(item))


def layer_kernel(
    got_ref, flat_ref, cotangent_ref, weight_ref, bias_ref, z_ref, y_ref, yt_ref, rep_ref,
    output_ref, hidden_ref, send_ref, held_ref, e2_ref, p1_ref, sums_ref, sems, *, pieces, loops, cells_y,
):
    rows = z_ref.shape[0]
    width = rep_ref.shape[0]
    rows_x = cotangent_ref.shape[1]
    lanes = flat_ref.shape[1] // pieces
    expand_y(got_ref, yt_ref, sums_ref, e2_ref, cells_y)
    mix = spread_weight(rep_ref, weight_ref[...].astype(F32).T.astype(BF16))
    bias = jnp.sum(rep_ref[...].astype(F32) * bias_ref[...], axis=1, keepdims=True)
    bias = jnp.broadcast_to(bias, (width, CHUNK))
    chunks = flat_ref.shape[1] // CHUNK // loops
    per = pieces // loops

    def send_piece(i):
        span = pl.ds(pl.multiple_of(i * lanes, lanes), lanes)
        return pltpu.make_async_copy(held_ref.at[:, :, span], output_ref.at[:, :, span], sems.at[0, i])

    def piece(i, total):
        base = pl.multiple_of(i * (chunks * YC * PITCH), 8)
        z = z_ref[...]
        totals = [total]

        def lanes_of(j):
            return pl.ds(pl.multiple_of((i * chunks + j) * CHUNK, CHUNK), CHUNK)

        def turn(j, _):
            return take_chunk(e2_ref, base, j).T

        def evaluate(j, e2):
            left = jnp.concatenate([e2, mix], 1)
            return dot(left, jnp.concatenate([z, flat_ref[:, lanes_of(j)]], 0)) + bias

        def activate(j, pre):
            own = lanes_of(j)
            square = pre * pre
            half = 0.5 * jnp.tanh(pre * (GELU_A + GELU_B * square)) + 0.5
            held_ref[:, :, own] = (pre * half).astype(BF16).reshape(-1, rows_x, CHUNK)
            slope = half + (half - half * half) * (pre * (2 * GELU_A + 6 * GELU_B * square))
            cot = cotangent_ref[:, :, own].reshape(-1, CHUNK).astype(F32)
            hidden = (cot * slope).astype(BF16)
            hidden_ref[:, own] = hidden
            if (j + 1) % (chunks // per) == 0:
                send_piece(i * per + j // (chunks // per)).start()
            return hidden

        def reduce(j, hidden):
            cells = flat_ref[:, lanes_of(j)]
            sums = dot(jnp.concatenate([z, cells], 0), hidden, NT)
            put_chunk(p1_ref, base, j, sums[:rows])
            totals[0] = totals[0] + sums[rows:]

        staged(chunks, [turn, evaluate, activate, reduce])
        return totals[0]

    total = [lax.fori_loop(0, loops, piece, jnp.zeros((width, width), F32))]
    contract_y(p1_ref, y_ref, sums_ref, cells_y)
    full = total[0]
    flat_row = jnp.sum(p1_ref[pl.ds(0, cells_y, stride=PITCH), :], axis=0, keepdims=True)
    flat_row = jnp.broadcast_to(flat_row / z_ref[0:1, 0:1].astype(F32), (8, width))
    row = lax.broadcasted_iota(jnp.int32, full.shape, 0)
    col = lax.broadcasted_iota(jnp.int32, full.shape, 1)
    full = jnp.where(row % rows_x == col % rows_x, full, 0.0)
    rep = rep_ref[...].astype(F32)
    high = lax.Precision.HIGHEST
    tall = dot(jnp.concatenate([full, flat_row], 0), rep, precision=high)
    channels = rep.shape[1]
    local = dot(rep.T, tall[:width], precision=high)
    tops = [local[i : i + 8] for i in range(0, channels, 8)]
    bias_sum = jnp.broadcast_to(tall[width : width + 1], (8, channels))
    high = bias_sum.astype(BF16).astype(F32)
    blank = jnp.zeros((8, 128 - 2 * channels), F32)
    packed = jnp.concatenate(
        [jnp.concatenate(tops, 1), jnp.concatenate([high, bias_sum - high, blank], 1)], 0
    ).astype(BF16)
    devices = send_ref.shape[0]
    mode_rows = K * K // devices
    for d in range(devices):
        send_ref[d, :mode_rows] = block_of(sums_ref, d, mode_rows)
        send_ref[d, mode_rows:] = packed
    for i in range(pieces):
        send_piece(i).wait()


def field_grad_kernel(
    got_ref, hidden_any, weight_ref, z_ref, yt_ref, rep_ref, output_ref, hidden_ref, held_ref, e2_ref, sums_ref, sems,
    *, cells_y,
):
    rows_x = held_ref.shape[1]
    cells = hidden_ref.shape[1]
    takes = {}
    for k, (first, end) in enumerate(spans_of(PIECES, cells)):
        takes[first // CHUNK] = pltpu.make_async_copy(
            hidden_any.at[:, first:end], hidden_ref.at[:, first:end], sems.at[1, k]
        )
    sends = {}
    for k, (first, end) in enumerate(spans_of(PIECES, cells)):
        sends[end // CHUNK - 1] = pltpu.make_async_copy(
            held_ref.at[:, :, first:end], output_ref.at[:, :, first:end], sems.at[0, k]
        )
    for take in takes.values():
        take.start()
    expand_y(got_ref, yt_ref, sums_ref, e2_ref, cells_y)
    mix = spread_weight(rep_ref, weight_ref[...])
    z = z_ref[...]

    def turn(j, _):
        return take_chunk(e2_ref, 0, j).T

    def evaluate(j, e2):
        left = jnp.concatenate([e2, mix], 1)
        own = slice(j * CHUNK, (j + 1) * CHUNK)
        if j in takes:
            takes[j].wait()
        grad = dot(left, jnp.concatenate([z, hidden_ref[:, own]], 0))
        held_ref[:, :, own] = grad.astype(BF16).reshape(-1, rows_x, CHUNK)
        if j in sends:
            sends[j].start()

    staged(cells // CHUNK, [turn, evaluate])
    for send in sends.values():
        send.wait()


def body(state_field, cotangent, spectral_weight, local_weight, local_bias):
    channels, rows_x, cells = state_field.shape
    cells_y = cells // NZ
    devices = lax.axis_size("gx")
    mode_rows = spectral_weight.shape[1]
    wide = channels * rows_x
    groups = K // AG
    table = tables(channels, rows_x, devices, cells_y)
    in_vmem = pl.BlockSpec(memory_space=pltpu.VMEM)

    def params(mib):
        return pltpu.CompilerParams(vmem_limit_bytes=mib * 1024 * 1024)

    in_any = pl.BlockSpec(memory_space=pl.ANY)
    held = pltpu.VMEM((channels, rows_x, cells), BF16)
    sems = pltpu.SemaphoreType.DMA((2, PIECES))
    field = jax.ShapeDtypeStruct(state_field.shape, BF16)
    flat_field = jax.ShapeDtypeStruct((wide, cells), BF16)

    def cost(moved):
        return pl.CostEstimate(flops=0, bytes_accessed=moved, transcendentals=0)

    blocks = jax.ShapeDtypeStruct((devices, mode_rows, wide), BF16)
    packed = jax.ShapeDtypeStruct((devices, mode_rows + PACK, wide), BF16)
    coeffs_shape = jax.ShapeDtypeStruct((groups * mode_rows, AG * channels), F32)
    p1 = pltpu.VMEM((cells_y * PITCH, wide), F32)
    sums = pltpu.VMEM((K * PITCH, wide), F32)
    weight = spectral_weight.reshape(groups, AG, mode_rows, channels * channels)

    def exchange(values_in):
        return lax.all_to_all(values_in, "gx", 0, 0, tiled=True)

    def in_hbm(array):
        return pltpu.with_memory_space_constraint(array, pltpu.HBM)

    projected, flat, x_table = pl.pallas_call(
        functools.partial(project_kernel, cells_y=cells_y),
        in_specs=[in_any] * 4,
        out_specs=[in_vmem] * 3,
        out_shape=[blocks, flat_field, jax.ShapeDtypeStruct(table["x"].shape, BF16)],
        scratch_shapes=[
            pltpu.VMEM(table["z"].shape, BF16), pltpu.VMEM(table["y"].shape, BF16),
            held, p1, sums, pltpu.SemaphoreType.DMA((5,)),
        ],
        compiler_params=params(18),
        cost_estimate=cost(48 << 20),
        name="project",
    )(in_hbm(state_field), in_hbm(table["z"]), in_hbm(table["y"]), in_hbm(table["x"]))
    got = exchange(projected)
    mixed, coeffs = pl.pallas_call(
        mix_kernel,
        in_specs=[in_vmem] * 3,
        out_specs=[in_vmem] * 2,
        out_shape=[blocks, coeffs_shape],
        compiler_params=params(10),
        cost_estimate=cost(48 << 20),
        name="mix",
    )(got, weight, x_table)
    got = exchange(mixed)
    bias_row = local_bias.reshape(1, channels)
    layer_output, hidden, projected = pl.pallas_call(
        functools.partial(layer_kernel, pieces=PIECES, loops=2, cells_y=cells_y),
        in_specs=[in_vmem] * 9,
        out_specs=[in_any, in_vmem, in_vmem],
        out_shape=[field, flat_field, packed],
        scratch_shapes=[held, p1, p1, sums, sems],
        compiler_params=params(22),
        cost_estimate=cost(64 << 20),
        name="layer",
    )(
        got, flat, cotangent, local_weight, bias_row,
        table["z"], table["y"], table["yt"], table["rep"],
    )
    got = exchange(projected)
    back, grads, local, bias_grad = pl.pallas_call(
        back_kernel,
        in_specs=[in_vmem] * 3,
        out_specs=[in_vmem] * 4,
        out_shape=[
            blocks, coeffs_shape,
            jax.ShapeDtypeStruct((channels, channels), F32), jax.ShapeDtypeStruct((1, channels), F32),
        ],
        compiler_params=params(10),
        cost_estimate=cost(48 << 20),
        name="back",
    )(got, weight, x_table)
    got = exchange(back)
    pairs = channels * channels
    spectral_grad = pl.pallas_call(
        spectral_kernel,
        grid=(AG,),
        in_specs=[in_vmem, in_vmem],
        out_specs=pl.BlockSpec((groups, 1, mode_rows, pairs), lambda i: (0, i, 0, 0)),
        out_shape=jax.ShapeDtypeStruct((groups, AG, mode_rows, pairs), F32),
        compiler_params=params(10),
        cost_estimate=pl.CostEstimate(
            flops=2 * 256 * K * mode_rows * pairs, bytes_accessed=4 * K * mode_rows * pairs, transcendentals=0
        ),
        name="spectral",
    )(coeffs, grads)
    field_grad = pl.pallas_call(
        functools.partial(field_grad_kernel, cells_y=cells_y),
        in_specs=[in_vmem, in_any] + [in_vmem] * 4,
        out_specs=in_any,
        out_shape=field,
        scratch_shapes=[pltpu.VMEM((wide, cells), BF16), held, p1, sums, sems],
        compiler_params=params(16),
        cost_estimate=cost(48 << 20),
        name="field_grad",
    )(got, in_hbm(hidden), local_weight, table["z"], table["yt"], table["rep"])
    spectral_grad = spectral_grad.reshape(K, mode_rows, pairs)
    return (layer_output, field_grad, spectral_grad, local, bias_grad.reshape(channels))


def solution(mesh):
    placed = (P(None, "gx", "grp"), P(None, "gx", "grp"), P(None, "gx", None), P(), P())
    return jax.shard_map(
        body,
        mesh=mesh,
        in_specs=placed,
        out_specs=(
            P(None, "gx", "grp"),
            P(None, "gx", "grp"),
            P("grp", "gx", None),
            P("grp", None),
            P("grp"),
        ),
        check_vma=False,
    )
```
